256 devices in a mesh: pipe: 2 (over z_lo), replica: 32 (over x, y, core), space: 4 (over z_hi).
Axes of the slice: x: 4, y: 4, z: 8 (z_hi: 4, z_lo: 2; z = z_hi * 2 + z_lo), core: 2. Of those that a mesh axis runs over, the one named last changes fastest.
Arguments:
- views: bfloat16 [2, 32, 32, 100, 176], P('pipe', 'replica', 'space'), may hold values from -1.6953125 to 1.6953125
- w_expand: bfloat16 [2, 176, 1056], P('pipe'), may hold values from -0.12988281 to 0.12988281
- w_depth: bfloat16 [2, 5, 5, 1056], P('pipe'), may hold values from -0.34960938 to 0.34960938
- w_reduce: bfloat16 [2, 1056, 44], P('pipe'), may hold values from -0.19921875 to 0.19921875
- w_excite: bfloat16 [2, 44, 1056], P('pipe'), may hold values from -0.5 to 0.5
- w_project: bfloat16 [2, 1056, 176], P('pipe'), may hold values from -0.052978516 to 0.052978516
- w_head: bfloat16 [2, 176, 5504], P('pipe'), may hold values from -0.12988281 to 0.12988281
- w_class: bfloat16 [2, 5504, 500], P('pipe'), may hold values from -0.22949219 to 0.22949219
Outputs:
- g_expand: float32 [2, 176, 1056], P('pipe')
- g_depth: float32 [2, 5, 5, 1056], P('pipe')
- g_reduce: float32 [2, 1056, 44], P('pipe')
- g_excite: float32 [2, 44, 1056], P('pipe')
- g_project: float32 [2, 1056, 176], P('pipe')
The draws below stay inside these ranges and needn't reach their ends.
All inputs are finite; a program needn't handle non-finite values.
Results may differ from the reference program's by a relative error of at most 0.0065.
Values may be sent and summed in bfloat16 or wider, within the bound.
No kernel may reach another device: no remote copies, remote signals or barrier semaphores. Data moves between devices by JAX's collectives and lax.ppermute only.
A program may use at most 128 MiB of HBM per device.

```python
from functools import reduce
import jax
import jax.numpy as jnp
from jax import lax

C = 176
E = 1056
R = 44
F = 5504
K = 500
KS = 5
W = 100
H = 32
BATCH = 32


def block_scale(stream_key, shape, shards, least, largest):
    loudness = 1.0
    for position, parts in shards:
        draws = jax.random.uniform(jax.random.fold_in(jax.random.fold_in(stream_key, 6), position), (parts,), jnp.float32, least / len(shards), largest / len(shards))
        loudness = loudness * jnp.repeat(jnp.exp(draws), shape[position] // parts).reshape((-1,) + (1,) * (len(shape) - 1 - position))
    return loudness


def setup_inputs(seed: int = 0) -> dict:
    keys = jax.random.split(jax.random.key(seed), 9)
    return {
        "views": jnp.clip(jax.random.uniform(keys[0], (2, BATCH, H, W, C), jnp.float32, -1.6953125, 1.6953125) * block_scale(keys[0], (2, BATCH, H, W, C), ((0, 2), (1, 32), (2, 4)), -0.4, 0.0), -1.6953125, 1.6953125).astype(jnp.bfloat16),
        "w_expand": jnp.clip(jax.random.uniform(keys[1], (2, C, E), jnp.float32, -0.12988281, 0.12988281) * block_scale(keys[1], (2, C, E), ((0, 2),), -0.4, 0.0), -0.12988281, 0.12988281).astype(jnp.bfloat16),
        "w_depth": jnp.clip(jax.random.uniform(keys[2], (2, KS, KS, E), jnp.float32, -0.34960938, 0.34960938) * block_scale(keys[2], (2, KS, KS, E), ((0, 2),), -0.4, 0.0), -0.34960938, 0.34960938).astype(jnp.bfloat16),
        "w_reduce": jnp.clip(jax.random.uniform(keys[3], (2, E, R), jnp.float32, -0.19921875, 0.19921875) * block_scale(keys[3], (2, E, R), ((0, 2),), -0.4, 0.0), -0.19921875, 0.19921875).astype(jnp.bfloat16),
        "w_excite": jnp.clip(jax.random.uniform(keys[4], (2, R, E), jnp.float32, -0.5, 0.5) * block_scale(keys[4], (2, R, E), ((0, 2),), -0.4, 0.0), -0.5, 0.5).astype(jnp.bfloat16),
        "w_project": jnp.clip(jax.random.uniform(keys[5], (2, E, C), jnp.float32, -0.052978516, 0.052978516) * block_scale(keys[5], (2, E, C), ((0, 2),), -0.4, 0.0), -0.052978516, 0.052978516).astype(jnp.bfloat16),
        "w_head": jnp.clip(jax.random.uniform(keys[6], (2, C, F), jnp.float32, -0.12988281, 0.12988281) * block_scale(keys[6], (2, C, F), ((0, 2),), -0.4, 0.0), -0.12988281, 0.12988281).astype(jnp.bfloat16),
        "w_class": jnp.clip(jax.random.uniform(keys[7], (2, F, K), jnp.float32, -0.22949219, 0.22949219) * block_scale(keys[7], (2, F, K), ((0, 2),), -0.4, 0.0), -0.22949219, 0.22949219).astype(jnp.bfloat16),
    }


loss_scale = 256.0
highest = lax.Precision.HIGHEST

def swish_act(value):
    return value * jax.nn.sigmoid(value)

def swish_slope(value):
    sigma = jax.nn.sigmoid(value)
    return sigma * (1.0 + value * (1.0 - sigma))

def depthwise(padded, kernel, height, breadth):
    extent = kernel.shape[0]
    pieces = [padded[..., step_y:step_y + height, step_x:step_x + breadth, :].astype(jnp.float32) * kernel[step_y, step_x].astype(jnp.float32) for step_y in range(extent) for step_x in range(extent)]
    return reduce(lambda left, right: left + right, pieces)

def transposed(padded, kernel, height, breadth):
    extent = kernel.shape[0]
    pieces = [padded[..., extent - 1 - step_y:extent - 1 - step_y + height, extent - 1 - step_x:extent - 1 - step_x + breadth, :].astype(jnp.float32) * kernel[step_y, step_x].astype(jnp.float32) for step_y in range(extent) for step_x in range(extent)]
    return reduce(lambda left, right: left + right, pieces)

def kernel_grad(gradient, padded, height, breadth, extent):
    axes_all = tuple(range(gradient.ndim - 1))
    grad_wide = gradient.astype(jnp.float32)
    stacked = [jnp.stack([lax.optimization_barrier(jnp.sum(grad_wide * padded[..., step_y:step_y + height, step_x:step_x + breadth, :].astype(jnp.float32), axis=axes_all)) for step_x in range(extent)]) for step_y in range(extent)]
    return jnp.stack(stacked)

def forward(params, image):
    expand_w, depth_w, reduce_w, excite_w, project_w, head_w, class_w = params
    height, breadth, channels = image.shape
    cell_total = height * breadth
    margin = depth_w.shape[0] // 2
    flat_view = image.reshape(cell_total, channels)
    pre_expand = jnp.dot(flat_view, expand_w, preferred_element_type=jnp.float32).reshape(height, breadth, -1)
    expanded = swish_act(pre_expand).astype(jnp.bfloat16)
    padded_exp = jnp.pad(expanded, ((margin, margin), (margin, margin), (0, 0)))
    pre_depth = depthwise(padded_exp, depth_w, height, breadth)
    act_depth = swish_act(pre_depth)
    squeeze = lax.optimization_barrier(jnp.sum(act_depth, axis=(0, 1))) / cell_total
    reduced_in = jnp.dot(squeeze, reduce_w.astype(jnp.float32), precision=highest)
    reduced = swish_act(reduced_in)
    excite_gate = jax.nn.sigmoid(jnp.dot(reduced, excite_w.astype(jnp.float32), precision=highest))
    gated = (act_depth * excite_gate).astype(jnp.bfloat16)
    flat_gated = gated.reshape(cell_total, -1)
    block_out = (flat_view.astype(jnp.float32) + jnp.dot(flat_gated, project_w, preferred_element_type=jnp.float32)).astype(jnp.bfloat16)
    pre_head = jnp.dot(block_out, head_w, preferred_element_type=jnp.float32)
    pooled = (lax.optimization_barrier(jnp.sum(swish_act(pre_head), axis=0)) / cell_total).astype(jnp.bfloat16)
    logits = jnp.dot(pooled, class_w, preferred_element_type=jnp.float32)
    stored = (flat_view, pre_expand, padded_exp, pre_depth, act_depth, squeeze, reduced_in, reduced, excite_gate, flat_gated, pre_head)
    return (logits, stored)

def backward(params, stored, grad_logits):
    expand_w, depth_w, reduce_w, excite_w, project_w, head_w, class_w = params
    flat_view, pre_expand, padded_exp, pre_depth, act_depth, squeeze, reduced_in, reduced, excite_gate, flat_gated, pre_head = stored
    height, breadth, hidden = pre_depth.shape
    cell_total = height * breadth
    extent = depth_w.shape[0]
    margin = extent // 2
    grad_pooled = jnp.dot(class_w, grad_logits, preferred_element_type=jnp.float32)
    grad_head = (grad_pooled / cell_total * swish_slope(pre_head)).astype(jnp.bfloat16)
    grad_block = jnp.dot(grad_head, head_w.T, preferred_element_type=jnp.float32).astype(jnp.bfloat16)
    g_project = jnp.dot(flat_gated.T, grad_block, preferred_element_type=jnp.float32)
    grad_gated = jnp.dot(grad_block, project_w.T, preferred_element_type=jnp.float32).reshape(height, breadth, hidden)
    grad_gate = lax.optimization_barrier(jnp.sum(grad_gated * act_depth, axis=(0, 1)))
    grad_excite = grad_gate * excite_gate * (1.0 - excite_gate)
    g_excite = jnp.outer(reduced, grad_excite)
    grad_reduced = jnp.dot(excite_w.astype(jnp.float32), grad_excite, precision=highest) * swish_slope(reduced_in)
    g_reduce = jnp.outer(squeeze, grad_reduced)
    back_pool = jnp.dot(reduce_w.astype(jnp.float32), grad_reduced, precision=highest)
    grad_act = grad_gated * excite_gate + back_pool / cell_total
    grad_depth = (grad_act * swish_slope(pre_depth)).astype(jnp.bfloat16)
    padded_grad = jnp.pad(grad_depth, ((margin, margin), (margin, margin), (0, 0)))
    g_depth = kernel_grad(grad_depth, padded_exp, height, breadth, extent)
    grad_expanded = transposed(padded_grad, depth_w, height, breadth)
    grad_expand = (grad_expanded * swish_slope(pre_expand)).astype(jnp.bfloat16)
    g_expand = jnp.dot(flat_view.T, grad_expand.reshape(cell_total, hidden), preferred_element_type=jnp.float32)
    return (g_expand, g_depth, g_reduce, g_excite, g_project)

def reference(views, w_expand, w_depth, w_reduce, w_excite, w_project, w_head, w_class):
    weights = (w_expand, w_depth, w_reduce, w_excite, w_project, w_head, w_class)
    teacher = tuple((weight[0] for weight in weights))
    student = tuple((weight[1] for weight in weights))

    def one_image(running, view_pair):
        teacher_view, student_view = view_pair
        teacher_logits, teacher_store = forward(teacher, teacher_view)
        student_logits, student_store = forward(student, student_view)
        exp_teacher = jnp.exp(teacher_logits)
        teacher_prob = exp_teacher / jnp.sum(exp_teacher)
        student_logprob = student_logits - jnp.log(jnp.sum(jnp.exp(student_logits)))
        cross = jnp.sum(teacher_prob * student_logprob)
        teacher_grad = (loss_scale * teacher_prob * (cross - student_logprob)).astype(jnp.bfloat16)
        student_grad = (loss_scale * (jnp.exp(student_logprob) - teacher_prob)).astype(jnp.bfloat16)
        from_teacher = backward(teacher, teacher_store, teacher_grad)
        from_student = backward(student, student_store, student_grad)
        updated = tuple((older + jnp.stack([first, second]) for older, first, second in zip(running, from_teacher, from_student)))
        return (updated, None)
    initial = tuple((jnp.zeros(weight.shape, jnp.float32) for weight in weights[:5]))
    totals, ignored = lax.scan(one_image, initial, (views[0], views[1]))
    return (totals[0], totals[1], totals[2], totals[3], totals[4])
```

```python
from functools import reduce

import jax
import jax.numpy as jnp
from jax import lax
from jax.sharding import Mesh
from jax.sharding import PartitionSpec as P

loss_scale = 256.0
highest = lax.Precision.HIGHEST


def with_halo(array, sides, width):
    for axis, dim in sides:
        size, length = (lax.axis_size(axis), array.shape[dim])
        up = [(i, (i + 1) % size) for i in range(size - 1)]
        down = [(j, i) for i, j in up]
        last = lax.slice_in_dim(array, length - width, length, axis=dim)
        first = lax.slice_in_dim(array, 0, width, axis=dim)
        before = lax.ppermute(last, axis, up)
        after = lax.ppermute(first, axis, down)
        array = jnp.concatenate([before, array, after], axis=dim)
    return array


def swapped(array, axis, stride):
    return lax.ppermute(array, axis, [(i, i ^ 1 << stride) for i in range(lax.axis_size(axis))])


def summed(packed):
    rows, breadth = packed.shape
    peers = lax.axis_size("x") * lax.axis_size("y")
    share = -(-rows // (2 * peers * 8)) * 8
    padded = jnp.pad(packed, ((0, 2 * peers * share - rows), (0, 0)))
    halves = padded.reshape(2, peers, share, breadth)
    core = lax.axis_index("core")
    swap = [(0, 1), (1, 0)]
    mine = lax.dynamic_index_in_dim(halves, core, 0, False)
    other = lax.dynamic_index_in_dim(halves, 1 - core, 0, False)
    half = mine + lax.ppermute(other, "core", swap)
    pieces = lax.all_to_all(half, ("x", "y"), 0, 0, tiled=True)
    piece = jnp.sum(pieces, axis=0)
    for step in (1, 2):
        piece = piece + lax.ppermute(
            piece, "space", [(i, i ^ step) for i in range(lax.axis_size("space"))]
        )
    copies = jnp.broadcast_to(piece[None], pieces.shape)
    gathered = lax.all_to_all(copies, ("x", "y"), 0, 0, tiled=True)
    remote = lax.ppermute(gathered, "core", swap)
    first = jnp.where(core == 0, gathered, remote)
    second = jnp.where(core == 0, remote, gathered)
    return jnp.concatenate([first, second]).reshape(2 * peers * share, breadth)[:rows]


def swish_act(value):
    return value * jax.nn.sigmoid(value)


def swish_slope(value):
    sigma = jax.nn.sigmoid(value)
    return sigma * (1.0 + value * (1.0 - sigma))


def depthwise(padded, kernel, height, breadth):
    extent = kernel.shape[0]
    pieces = [
        padded[..., step_y : step_y + height, step_x : step_x + breadth, :].astype(jnp.float32)
        * kernel[step_y, step_x].astype(jnp.float32)
        for step_y in range(extent)
        for step_x in range(extent)
    ]
    return reduce(lambda left, right: left + right, pieces)


def transposed(padded, kernel, height, breadth):
    extent = kernel.shape[0]
    pieces = [
        padded[
            ...,
            extent - 1 - step_y : extent - 1 - step_y + height,
            extent - 1 - step_x : extent - 1 - step_x + breadth,
            :,
        ].astype(jnp.float32)
        * kernel[step_y, step_x].astype(jnp.float32)
        for step_y in range(extent)
        for step_x in range(extent)
    ]
    return reduce(lambda left, right: left + right, pieces)


def kernel_grad(gradient, padded, height, breadth, extent):
    axes_all = tuple(range(gradient.ndim - 1))
    grad_wide = gradient.astype(jnp.float32)
    stacked = [
        jnp.stack(
            [
                jnp.sum(
                    grad_wide
                    * padded[..., step_y : step_y + height, step_x : step_x + breadth, :].astype(
                        jnp.float32
                    ),
                    axis=axes_all,
                )
                for step_x in range(extent)
            ]
        )
        for step_y in range(extent)
    ]
    return jnp.stack(stacked)


def shards(views, w_expand, w_depth, w_reduce, w_excite, w_project, w_head, w_class):
    own_view = views[0]
    expand_w = w_expand[0]
    depth_w = w_depth[0]
    reduce_w = w_reduce[0]
    excite_w = w_excite[0]
    project_w = w_project[0]
    head_w = w_head[0]
    class_w = w_class[0]
    images, row_count, col_count, channels = own_view.shape
    hidden = expand_w.shape[1]
    head_width = head_w.shape[1]
    extent = depth_w.shape[0]
    margin = extent // 2
    cell_total = row_count * lax.axis_size("space") * col_count
    flat_view = own_view.reshape(-1, channels)
    pre_expand = jnp.dot(flat_view, expand_w, preferred_element_type=jnp.float32).reshape(
        images, row_count, col_count, hidden
    )
    expanded = swish_act(pre_expand).astype(jnp.bfloat16)
    with_rim = with_halo(expanded, (("space", 1),), 2)
    padded_exp = jnp.pad(with_rim, ((0, 0), (0, 0), (margin, margin), (0, 0)))
    pre_depth = depthwise(padded_exp, depth_w, row_count, col_count)
    act_depth = swish_act(pre_depth)
    squeeze = lax.psum(jnp.sum(act_depth, axis=(1, 2)), "space") / cell_total
    reduced_in = jnp.dot(squeeze, reduce_w.astype(jnp.float32), precision=highest)
    reduced = swish_act(reduced_in)
    excite_gate = jax.nn.sigmoid(jnp.dot(reduced, excite_w.astype(jnp.float32), precision=highest))
    gated = (act_depth * excite_gate[:, None, None, :]).astype(jnp.bfloat16)
    flat_gated = gated.reshape(-1, hidden)
    block_out = (
        flat_view.astype(jnp.float32)
        + jnp.dot(flat_gated, project_w, preferred_element_type=jnp.float32)
    ).astype(jnp.bfloat16)
    pre_head = jnp.dot(block_out, head_w, preferred_element_type=jnp.float32)
    head_sum = jnp.sum(swish_act(pre_head).reshape(images, -1, head_width), axis=1)
    pooled = (lax.psum(head_sum, "space") / cell_total).astype(jnp.bfloat16)
    logits = jnp.dot(pooled, class_w, preferred_element_type=jnp.float32)
    partner = swapped(logits, "pipe", 0)
    teacher = lax.axis_index("pipe") == 0
    teacher_logits = jnp.where(teacher, logits, partner)
    student_logits = jnp.where(teacher, partner, logits)
    exp_teacher = jnp.exp(teacher_logits)
    teacher_prob = exp_teacher / jnp.sum(exp_teacher, axis=-1, keepdims=True)
    student_logprob = student_logits - jnp.log(
        jnp.sum(jnp.exp(student_logits), axis=-1, keepdims=True)
    )
    cross = jnp.sum(teacher_prob * student_logprob, axis=-1, keepdims=True)
    teacher_grad = loss_scale * teacher_prob * (cross - student_logprob)
    student_grad = loss_scale * (jnp.exp(student_logprob) - teacher_prob)
    grad_logits = jnp.where(teacher, teacher_grad, student_grad).astype(jnp.bfloat16)
    grad_pooled = jnp.einsum("ik,fk->if", grad_logits, class_w, preferred_element_type=jnp.float32)
    grad_head = (
        (
            grad_pooled[:, None, :]
            / cell_total
            * swish_slope(pre_head.reshape(images, -1, head_width))
        )
        .astype(jnp.bfloat16)
        .reshape(-1, head_width)
    )
    grad_block = jnp.einsum(
        "mf,cf->mc", grad_head, head_w, preferred_element_type=jnp.float32
    ).astype(jnp.bfloat16)
    g_project = jnp.einsum("me,mc->ec", flat_gated, grad_block, preferred_element_type=jnp.float32)
    grad_gated = jnp.einsum(
        "mc,ec->me", grad_block, project_w, preferred_element_type=jnp.float32
    ).reshape(images, row_count, col_count, hidden)
    grad_gate = lax.psum(jnp.sum(grad_gated * act_depth, axis=(1, 2)), "space")
    grad_excite = grad_gate * excite_gate * (1.0 - excite_gate)
    first_block = lax.axis_index("space") == 0
    g_excite = jnp.where(
        first_block, jnp.einsum("ir,ie->re", reduced, grad_excite, precision=highest), 0.0
    )
    grad_reduced = jnp.einsum(
        "ie,re->ir", grad_excite, excite_w.astype(jnp.float32), precision=highest
    ) * swish_slope(reduced_in)
    g_reduce = jnp.where(
        first_block, jnp.einsum("ie,ir->er", squeeze, grad_reduced, precision=highest), 0.0
    )
    back_pool = jnp.einsum(
        "ir,er->ie", grad_reduced, reduce_w.astype(jnp.float32), precision=highest
    )
    grad_act = (
        grad_gated * excite_gate[:, None, None, :] + (back_pool / cell_total)[:, None, None, :]
    )
    grad_depth = (grad_act * swish_slope(pre_depth)).astype(jnp.bfloat16)
    grad_rim = with_halo(grad_depth, (("space", 1),), 2)
    padded_grad = jnp.pad(grad_rim, ((0, 0), (0, 0), (margin, margin), (0, 0)))
    g_depth = kernel_grad(grad_depth, padded_exp, row_count, col_count, extent)
    grad_expanded = transposed(padded_grad, depth_w, row_count, col_count)
    grad_expand = (grad_expanded * swish_slope(pre_expand)).astype(jnp.bfloat16)
    g_expand = jnp.einsum(
        "mc,me->ce", flat_view, grad_expand.reshape(-1, hidden), preferred_element_type=jnp.float32
    )
    packed = jnp.concatenate(
        [
            g_expand,
            g_depth.reshape(extent * extent, hidden),
            g_reduce.T,
            g_excite,
            g_project.T,
        ]
    )
    marks = [0]
    for rows in (channels, extent * extent, reduce_w.shape[1], reduce_w.shape[1], channels):
        marks.append(marks[-1] + rows)
    total = summed(packed)
    parts = [total[start:stop] for start, stop in zip(marks, marks[1:])]
    return (
        parts[0][None],
        parts[1].reshape(1, extent, extent, hidden),
        parts[2].T[None],
        parts[3][None],
        parts[4].T[None],
    )


def solution(mesh):
    pipe, replica, space = (mesh.shape[name] for name in ("pipe", "replica", "space"))
    side = 1
    while 2 * side * side < replica:
        side *= 2
    fine = Mesh(
        mesh.devices.reshape(pipe, replica // (2 * side), side, 2, space),
        ("pipe", "x", "y", "core", "space"),
    )
    in_specs = (
        P("pipe", ("x", "y", "core"), "space", None, None),
        P("pipe", None, None),
        P("pipe", None, None, None),
        P("pipe", None, None),
        P("pipe", None, None),
        P("pipe", None, None),
        P("pipe", None, None),
        P("pipe", None, None),
    )
    out_specs = (
        P("pipe", None, None),
        P("pipe", None, None, None),
        P("pipe", None, None),
        P("pipe", None, None),
        P("pipe", None, None),
    )
    return jax.shard_map(shards, mesh=fine, in_specs=in_specs, out_specs=out_specs, check_vma=False)
```

```python
import jax
import jax.numpy as jnp
from jax import lax
from jax.experimental import pallas as pl
from jax.experimental.pallas import tpu as pltpu
from jax.sharding import Mesh
from jax.sharding import PartitionSpec as P

loss_scale = 256.0
f32 = jnp.float32
bf16 = jnp.bfloat16
LANES = 128
BAND = 384
HEAD_CHUNK = 512
STRIP = 20
VMEM = pl.BlockSpec(memory_space=pltpu.VMEM)
SMEM = pl.BlockSpec(memory_space=pltpu.SMEM)
ANY = pl.BlockSpec(memory_space=pl.ANY)


def up_to(size, multiple):
    return -(-size // multiple) * multiple


def params(**extra):
    return pltpu.CompilerParams(vmem_limit_bytes=50 * 1024 * 1024, **extra)


def contract(left, right, left_dim, right_dim):
    return lax.dot_general(
        left, right, (((left_dim,), (right_dim,)), ((), ())), preferred_element_type=f32
    )


def row_window(own, rim, extent, place):
    margin = extent // 2
    window = []
    for i in range(extent):
        d = i - margin
        if d == 0:
            window.append(own)
        elif d > 0:
            window.append(pltpu.roll(jnp.where(place < d, rim, own), 8 - d, 0))
        else:
            window.append(pltpu.roll(jnp.where(place >= 8 + d, rim, own), -d, 0))
    return window


def forward_kernel(
    own_ref, before_ref, after_ref, expand_ref, depth_ref,
    cells_ref, cells_t_ref, mine_ref, half_ref, squeeze_ref,
    left, right, expanded,
):
    columns, channels = own_ref.shape[1:]
    extent, margin = 5, 2

    @pl.when(pl.program_id(0) == 0)
    def lay_out():
        left[...] = jnp.zeros_like(left)
        right[...] = jnp.zeros_like(right)
        rest = channels - LANES
        for ref, first, base in ((own_ref, 0, 0), (after_ref, 0, 8), (before_ref, 0, 14)):
            for y in range(ref.shape[0]):
                row = ref[y].astype(f32)
                left[pl.ds(base + y, columns, stride=16), :] = row[:, :LANES]
                right[pl.ds(base + y, columns, stride=16), :] = jnp.concatenate(
                    [row[:, LANES:], jnp.zeros((columns, LANES - rest), f32)], axis=1
                )
        low, high = left[...], right[...]
        cells_ref[:, :LANES] = low.astype(bf16)
        cells_ref[:, LANES:] = high[:, :rest].astype(bf16)
        for start in range(0, 16 * columns, 320):
            cells_t_ref[:LANES, start : start + 320] = left[start : start + 320, :].T.astype(bf16)
            cells_t_ref[LANES:, start : start + 320] = right[start : start + 320, :].T[
                :rest
            ].astype(bf16)
        mine_ref[:, :LANES] = (
            low.reshape(columns, 16, LANES)[:, :8].reshape(8 * columns, LANES).astype(bf16)
        )
        mine_ref[:, LANES:] = (
            high.reshape(columns, 16, LANES)[:, :8]
            .reshape(8 * columns, LANES)[:, :rest]
            .astype(bf16)
        )
        edge = jnp.zeros((margin, 16, BAND), f32)
        expanded[:margin] = edge
        expanded[margin + columns :] = edge

    @pl.loop(0, columns // 10)
    def expand(part):
        cells = cells_ref[pl.ds(pl.multiple_of(part * 160, 160), 160), :]
        half = jnp.dot(cells, expand_ref[...], preferred_element_type=f32)
        value = half + half * jnp.tanh(half)
        expanded[pl.ds(margin + part * 10, 10)] = value.reshape(10, 16, BAND)

    place = lax.broadcasted_iota(jnp.int32, (8, LANES), 0)

    @pl.loop(0, BAND // LANES)
    def convolve(tile):
        lanes = pl.ds(pl.multiple_of(tile * LANES, LANES), LANES)
        weight = [
            [depth_ref[i * extent + j : i * extent + j + 1, lanes] for j in range(extent)]
            for i in range(extent)
        ]

        def strip(number, total):
            x0 = number * STRIP
            sums = {}
            for k in range(STRIP + extent - 1):
                window = row_window(
                    expanded[x0 + k, :8, lanes], expanded[x0 + k, 8:, lanes], extent, place
                )
                for j in range(extent):
                    x = k - j
                    if 0 <= x < STRIP:
                        term = window[0] * weight[0][j]
                        for i in range(1, extent):
                            term = term + window[i] * weight[i][j]
                        sums[x] = term if x not in sums else sums[x] + term
                x = k - extent + 1
                if x >= 0:
                    half = 0.5 * sums.pop(x)
                    half_ref[pl.ds(pl.multiple_of((x0 + x) * 8, 8), 8), lanes] = half
                    total = total + (half + half * jnp.tanh(half))
            return total

        total = lax.fori_loop(0, columns // STRIP, strip, jnp.zeros((8, LANES), f32))
        squeeze_ref[:, lanes] = jnp.sum(total, axis=0, keepdims=True)


def gate_of(squeeze, reduce_t, excite):
    reduced_in = jnp.sum(reduce_t * squeeze, axis=1, keepdims=True)
    reduced = reduced_in * jax.nn.sigmoid(reduced_in)
    gate = jax.nn.sigmoid(jnp.sum(excite * reduced, axis=0, keepdims=True))
    return reduced_in, reduced, gate


def head_kernel(
    half_ref, squeeze_ref, reduce_ref, excite_ref, project_ref, mine_ref, head_ref, class_ref,
    logits_ref, gated_ref, block_ref,
    gate_row, head_w, class_w, sums, sems,
):
    cells = half_ref.shape[0]
    width = head_ref.shape[1]
    classes = class_ref.shape[1]
    head_copy = pltpu.make_async_copy(head_ref, head_w.at[:, :width], sems.at[0])
    class_copy = pltpu.make_async_copy(class_ref, class_w, sems.at[1])
    head_copy.start()
    class_copy.start()
    head_w[:, width:] = jnp.zeros((head_w.shape[0], head_w.shape[1] - width), bf16)
    cell_total = 4 * cells
    gate_row[...] = gate_of(squeeze_ref[...] / cell_total, reduce_ref[...], excite_ref[...])[2]

    @pl.loop(0, cells // 80)
    def gating(part):
        rows = pl.ds(pl.multiple_of(part * 80, 80), 80)
        half = half_ref[rows, :]
        gated_ref[rows, :] = ((half + half * jnp.tanh(half)) * gate_row[...]).astype(bf16)

    residual = contract(gated_ref[...], project_ref[...], 1, 1)
    block = (mine_ref[...].astype(f32) + residual).astype(bf16)
    block_ref[...] = (0.5 * block.astype(f32)).astype(bf16)
    head_copy.wait()

    @pl.loop(0, head_w.shape[1] // HEAD_CHUNK)
    def head(part):
        lanes = pl.ds(pl.multiple_of(part * HEAD_CHUNK, HEAD_CHUNK), HEAD_CHUNK)
        half = jnp.dot(block_ref[...], head_w[:, lanes], preferred_element_type=f32)
        act = half + half * jnp.tanh(half)
        sums[:, lanes] = jnp.sum(act.reshape(cells // 8, 8, HEAD_CHUNK), axis=0)

    class_copy.wait()
    pooled = sums[:, :width]
    high = pooled.astype(bf16).astype(f32)
    both = jnp.concatenate([high, pooled - high], axis=0).astype(bf16)
    partial = jnp.sum(
        jnp.dot(both, class_w[...], preferred_element_type=f32), axis=0, keepdims=True
    )
    logits_ref[...] = jnp.zeros_like(logits_ref)
    logits_ref[:, :classes] = jnp.broadcast_to(
        partial / cell_total, (logits_ref.shape[0], classes)
    )


def head_grad_kernel(
    which_ref, logits_ref, block_ref, gated_ref, project_ref, head_ref, class_ref,
    grad_ref, project_grad_ref, gate_grad_ref,
    head_w, class_w, pooled, total, sems,
):
    cells = block_ref.shape[0]
    width = head_ref.shape[1]
    classes = class_ref.shape[1]
    head_copy = pltpu.make_async_copy(head_ref, head_w.at[:, :width], sems.at[0])
    class_copy = pltpu.make_async_copy(class_ref, class_w, sems.at[1])
    class_copy.start()
    head_copy.start()
    head_w[:, width:] = jnp.zeros((head_w.shape[0], head_w.shape[1] - width), bf16)
    total[...] = jnp.zeros_like(total)

    rows = logits_ref[...]
    network = lax.broadcasted_iota(jnp.int32, rows.shape, 0) % 2
    valid = lax.broadcasted_iota(jnp.int32, (1, rows.shape[1]), 1) < classes
    teacher = jnp.sum(jnp.where(network == 0, rows, 0.0), axis=0, keepdims=True)
    student = jnp.sum(jnp.where(network == 1, rows, 0.0), axis=0, keepdims=True)
    exp_teacher = jnp.where(valid, jnp.exp(teacher), 0.0)
    prob = exp_teacher / jnp.sum(exp_teacher, axis=1, keepdims=True)
    log_sum = jnp.log(
        jnp.sum(jnp.where(valid, jnp.exp(student), 0.0), axis=1, keepdims=True)
    )
    logprob = student - log_sum
    cross = jnp.sum(prob * logprob, axis=1, keepdims=True)
    teacher_grad = loss_scale * prob * (cross - logprob)
    student_grad = loss_scale * (jnp.exp(logprob) - prob)
    grad = jnp.where(which_ref[0] == 0, teacher_grad, student_grad)
    grad = jnp.where(valid, grad, 0.0)
    grad = jnp.broadcast_to(grad, (16, rows.shape[1])).astype(bf16)[:, :classes]
    class_copy.wait()
    pooled[:, :width] = contract(grad, class_w[...], 1, 1)[:1] * (0.5 / (4 * cells))
    pooled[:, width:] = jnp.zeros((1, pooled.shape[1] - width), f32)
    head_copy.wait()

    @pl.loop(0, head_w.shape[1] // HEAD_CHUNK)
    def head(part):
        lanes = pl.ds(pl.multiple_of(part * HEAD_CHUNK, HEAD_CHUNK), HEAD_CHUNK)
        weight = head_w[:, lanes]
        half = jnp.dot(block_ref[...], weight, preferred_element_type=f32)
        t = jnp.tanh(half)
        slope = (1.0 + t) * (1.0 + (half - half * t))
        grad_head = (slope * pooled[:, lanes]).astype(bf16)
        total[...] += contract(grad_head, weight, 1, 1)

    grad_block = total[...]
    grad_ref[...] = grad_block.astype(bf16)
    project_grad = jnp.dot(grad_block.T.astype(bf16), gated_ref[...], preferred_element_type=f32)
    project_grad_ref[...] = project_grad
    gate_grad_ref[...] = jnp.sum(
        project_ref[...].astype(f32) * project_grad, axis=0, keepdims=True
    )


def backward_kernel(
    space_ref, gate_grad_ref, squeeze_ref, reduce_ref, excite_ref, cells_ref, cells_t_ref,
    expand_ref, depth_ref, half_ref, grad_ref, project_ref, project_grad_ref,
    out_ref,
    gate_row, pool_row, excite_grad, reduce_grad, expanded, slope, grad_depth, grad_expand,
):
    step = pl.program_id(0)
    cells = half_ref.shape[0]
    columns = cells // 8
    channels = grad_ref.shape[1]
    reduced_rows = reduce_ref.shape[0]
    extent, margin = 5, 2
    cell_total = 4 * cells

    @pl.when(step == 0)
    def gates():
        squeeze = squeeze_ref[...] / cell_total
        reduced_in, reduced, gate = gate_of(squeeze, reduce_ref[...], excite_ref[...])
        grad_excite = (1.0 - gate) * gate_grad_ref[...]
        sigma = jax.nn.sigmoid(reduced_in)
        grad_reduced = jnp.sum(excite_ref[...] * grad_excite, axis=1, keepdims=True) * (
            sigma * (1.0 + reduced_in * (1.0 - sigma))
        )
        back_pool = jnp.sum(reduce_ref[...] * grad_reduced, axis=0, keepdims=True)
        gate_row[...] = 0.5 * gate
        pool_row[...] = back_pool * (0.5 / cell_total)
        once = jnp.where(space_ref[0] == 0, 1.0, 0.0)
        excite_grad[...] = reduced * (grad_excite * once)
        reduce_grad[...] = grad_reduced * (squeeze * once)
        edge = jnp.zeros((margin, 16, BAND), f32)
        expanded[:margin] = edge
        expanded[margin + columns :] = edge
        grad_depth[:margin] = edge[:, :8]
        grad_depth[margin + columns :] = edge[:, :8]

    band = pl.ds(pl.multiple_of(step * BAND, LANES), BAND)
    gate = gate_row[:, band]
    back_pool = pool_row[:, band]

    @pl.loop(0, columns // 10)
    def elements(part):
        rows = pl.ds(pl.multiple_of(part * 160, 160), 160)
        half = jnp.dot(cells_ref[rows, :], expand_ref[...], preferred_element_type=f32)
        t = jnp.tanh(half)
        turn = half * t
        expanded[pl.ds(margin + part * 10, 10)] = (half + turn).reshape(10, 16, BAND)
        slope[pl.ds(part * 10, 10)] = ((1.0 + t) * (1.0 + (half - turn))).reshape(10, 16, BAND)
        rows = pl.ds(pl.multiple_of(part * 80, 80), 80)
        grad_gated = jnp.dot(grad_ref[rows, :], project_ref[...], preferred_element_type=f32)
        half = half_ref[rows, :]
        t = jnp.tanh(half)
        value = (grad_gated * gate + back_pool) * ((1.0 + t) * (1.0 + (half - half * t)))
        grad_depth[pl.ds(margin + part * 10, 10)] = value.reshape(10, 8, BAND)

    place = lax.broadcasted_iota(jnp.int32, (8, LANES), 0)

    depth_base = 2 * channels
    excite_base = depth_base + up_to(extent * extent, 8)
    reduce_base = excite_base + reduced_rows
    out_ref[excite_base:reduce_base, :] = excite_grad[:, band]
    out_ref[reduce_base : reduce_base + reduced_rows, :] = reduce_grad[:, band]
    out_ref[channels:depth_base, :] = project_grad_ref[...]
    spare = out_ref.shape[0] - reduce_base - reduced_rows
    out_ref[reduce_base + reduced_rows :, :] = jnp.zeros((spare, BAND), f32)

    @pl.loop(0, BAND // LANES)
    def convolve(tile):
        lanes = pl.ds(pl.multiple_of(tile * LANES, LANES), LANES)

        def taps(number, sums):
            sums = [list(line) for line in sums]
            base = margin + number * 10
            grads = {}
            for k in range(10):
                window = row_window(
                    expanded[base + k, :8, lanes], expanded[base + k, 8:, lanes], extent, place
                )
                for j in range(extent):
                    place_x = k - j
                    if place_x not in grads:
                        grads[place_x] = grad_depth[base + place_x + margin, :, lanes]
                    for i in range(extent):
                        sums[i][j] = sums[i][j] + window[i] * grads[place_x]
            return tuple(tuple(line) for line in sums)

        zero = jnp.zeros((8, LANES), f32)
        sums = lax.fori_loop(0, columns // 10, taps, ((zero,) * extent,) * extent)
        for i in range(extent):
            for j in range(extent):
                row = depth_base + i * extent + j
                out_ref[row : row + 1, lanes] = jnp.sum(sums[i][j], axis=0, keepdims=True)
        for row in range(depth_base + extent * extent, excite_base):
            out_ref[row : row + 1, lanes] = jnp.zeros((1, LANES), f32)

        weight = [
            [0.5 * depth_ref[i * extent + j : i * extent + j + 1, lanes] for j in range(extent)]
            for i in range(extent)
        ]

        @pl.loop(0, columns // STRIP)
        def spread(number):
            x0 = number * STRIP
            grads = [grad_depth[x0 + k, :, lanes] for k in range(extent - 1)]
            for x in range(STRIP):
                grads.append(grad_depth[x0 + x + extent - 1, :, lanes])
                near, far = None, None
                for i in range(extent):
                    term = grads[x + extent - 1] * weight[i][0]
                    for j in range(1, extent):
                        term = term + grads[x + extent - 1 - j] * weight[i][j]
                    d = i - margin
                    if d == 0:
                        near = term if near is None else near + term
                        continue
                    rolled = pltpu.roll(term, d % 8, 0)
                    inside = place >= d if d > 0 else place < 8 + d
                    stay = jnp.where(inside, rolled, 0.0)
                    leave = jnp.where(inside, 0.0, rolled)
                    near = stay if near is None else near + stay
                    far = leave if far is None else far + leave
                near = near * slope[x0 + x, :8, lanes]
                far = far * slope[x0 + x, 8:, lanes]
                rows = pl.ds(pl.multiple_of((x0 + x) * 16, 16), 16)
                grad_expand[rows, lanes] = jnp.concatenate([near, far], axis=0).astype(bf16)

    out_ref[:channels, :] = jnp.dot(
        cells_t_ref[...], grad_expand[...], preferred_element_type=f32
    )


def unpack_kernel(
    core_ref, own_ref, other_ref, expand_ref, depth_ref, reduce_ref, excite_ref, project_ref
):
    channels, hidden = expand_ref.shape[1:]
    extent = depth_ref.shape[1]
    reduced = excite_ref.shape[1]
    depth_base = 2 * channels
    excite_base = depth_base + up_to(extent * extent, 8)
    reduce_base = excite_base + up_to(reduced, 8)
    half_rows = own_ref.shape[0]

    def rows(start, stop):
        pieces = []
        if start < half_rows:
            end = min(stop, half_rows)
            pieces.append(
                jnp.where(core_ref[0] == 0, own_ref[start:end, :], other_ref[start:end, :])
            )
        if stop > half_rows:
            begin = max(start, half_rows)
            pieces.append(
                jnp.where(
                    core_ref[0] == 0,
                    other_ref[begin - half_rows : stop - half_rows, :],
                    own_ref[begin - half_rows : stop - half_rows, :],
                )
            )
        return pieces[0] if len(pieces) == 1 else jnp.concatenate(pieces, axis=0)

    expand_ref[0] = rows(0, channels)[:, :hidden]
    project_ref[0] = rows(channels, depth_base).T[:hidden]
    depth = rows(depth_base, excite_base)
    for i in range(extent):
        depth_ref[0, i] = depth[i * extent : (i + 1) * extent, :hidden]
    excite_ref[0] = rows(excite_base, reduce_base)[:reduced, :hidden]
    reduce_ref[0] = rows(reduce_base, reduce_base + up_to(reduced, 8)).T[:hidden, :reduced]


def shards(views, w_expand, w_depth, w_reduce, w_excite, w_project, w_head, w_class):
    own = views[0, 0]
    height, columns, channels = own.shape
    hidden = w_expand.shape[2]
    reduced = w_reduce.shape[2]
    extent = w_depth.shape[1]
    width = w_head.shape[2]
    classes = w_class.shape[2]
    cells = height * columns
    space = lax.axis_size("space")
    broad = up_to(hidden, BAND)
    bands = broad // BAND
    tall = up_to(reduced, 8)

    up = [(i, i + 1) for i in range(space - 1)]
    down = [(i + 1, i) for i in range(space - 1)]
    before = lax.ppermute(own[height - 2 :], "space", up)
    after = lax.ppermute(own[:2], "space", down)

    fill = broad - hidden
    expand_w = jnp.pad(w_expand[0] * bf16(0.5), ((0, 0), (0, fill)))
    depth_w = jnp.pad(
        w_depth[0].reshape(extent * extent, hidden).astype(f32),
        ((0, up_to(extent * extent, 8) - extent * extent), (0, fill)),
    )
    reduce_t = jnp.pad(w_reduce[0].T.astype(f32), ((0, tall - reduced), (0, fill)))
    excite_w = jnp.pad(w_excite[0].astype(f32), ((0, tall - reduced), (0, fill)))
    project_t = jnp.pad(w_project[0].T, ((0, 0), (0, fill)))

    def whole(*shape):
        return pl.BlockSpec(shape, lambda e: (0,) * len(shape))

    def banded(rows):
        return pl.BlockSpec((rows, BAND), lambda e: (0, e))

    depth_rows = depth_w.shape[0]
    cell_rows, cells_t, mine, half, squeeze = pl.pallas_call(
        forward_kernel,
        grid=(bands,),
        in_specs=[
            whole(height, columns, channels),
            whole(2, columns, channels),
            whole(2, columns, channels),
            banded(channels),
            banded(depth_rows),
        ],
        out_specs=[
            whole(16 * columns, channels),
            whole(channels, 16 * columns),
            whole(cells, channels),
            banded(cells),
            banded(1),
        ],
        out_shape=[
            jax.ShapeDtypeStruct((16 * columns, channels), bf16),
            jax.ShapeDtypeStruct((channels, 16 * columns), bf16),
            jax.ShapeDtypeStruct((cells, channels), bf16),
            jax.ShapeDtypeStruct((cells, broad), f32),
            jax.ShapeDtypeStruct((1, broad), f32),
        ],
        scratch_shapes=[
            pltpu.VMEM((16 * columns, LANES), f32),
            pltpu.VMEM((16 * columns, LANES), f32),
            pltpu.VMEM((columns + 4, 16, BAND), f32),
        ],
        compiler_params=params(),
        name="expand_depthwise",
    )(own, before, after, expand_w, depth_w)
    squeeze = lax.psum(squeeze, "space")

    head_wide = up_to(width, HEAD_CHUNK)
    ranks = 2 * space
    logits, gated, block = pl.pallas_call(
        head_kernel,
        in_specs=[VMEM] * 6 + [ANY] * 2,
        out_specs=[VMEM] * 3,
        out_shape=[
            jax.ShapeDtypeStruct((ranks, up_to(classes, LANES)), f32),
            jax.ShapeDtypeStruct((cells, broad), bf16),
            jax.ShapeDtypeStruct((cells, channels), bf16),
        ],
        scratch_shapes=[
            pltpu.VMEM((1, broad), f32),
            pltpu.VMEM((channels, head_wide), bf16),
            pltpu.VMEM((width, classes), bf16),
            pltpu.VMEM((8, head_wide), f32),
            pltpu.SemaphoreType.DMA((2,)),
        ],
        compiler_params=params(),
        name="project_head",
    )(half, squeeze, reduce_t, excite_w, project_t, mine, w_head[0], w_class[0])
    logits = lax.all_to_all(logits, ("space", "pipe"), 0, 0, tiled=True)

    def index(name):
        return lax.axis_index(name).astype(jnp.int32).reshape(1)

    grad_block, project_grad, gate_grad = pl.pallas_call(
        head_grad_kernel,
        in_specs=[SMEM] + [VMEM] * 4 + [ANY] * 2,
        out_specs=[VMEM] * 3,
        out_shape=[
            jax.ShapeDtypeStruct((cells, channels), bf16),
            jax.ShapeDtypeStruct((channels, broad), f32),
            jax.ShapeDtypeStruct((1, broad), f32),
        ],
        scratch_shapes=[
            pltpu.VMEM((channels, head_wide), bf16),
            pltpu.VMEM((width, classes), bf16),
            pltpu.VMEM((1, head_wide), f32),
            pltpu.VMEM((cells, channels), f32),
            pltpu.SemaphoreType.DMA((2,)),
        ],
        compiler_params=params(),
        name="head_grad",
    )(index("pipe"), logits, block, gated, project_t, w_head[0], w_class[0])
    gate_grad = lax.psum(gate_grad, "space")

    peers = lax.axis_size("x") * lax.axis_size("y")
    used = 2 * channels + depth_rows + 2 * tall
    share = up_to(-(-used // (2 * peers)), 8)
    rows = 2 * peers * share
    packed = pl.pallas_call(
        backward_kernel,
        grid=(bands,),
        in_specs=[
            SMEM,
            whole(1, broad),
            whole(1, broad),
            whole(tall, broad),
            whole(tall, broad),
            whole(16 * columns, channels),
            whole(channels, 16 * columns),
            banded(channels),
            banded(depth_rows),
            banded(cells),
            whole(cells, channels),
            banded(channels),
            banded(channels),
        ],
        out_specs=banded(rows),
        out_shape=jax.ShapeDtypeStruct((rows, broad), f32),
        scratch_shapes=[
            pltpu.VMEM((1, broad), f32),
            pltpu.VMEM((1, broad), f32),
            pltpu.VMEM((tall, broad), f32),
            pltpu.VMEM((tall, broad), f32),
            pltpu.VMEM((columns + 4, 16, BAND), f32),
            pltpu.VMEM((columns, 16, BAND), f32),
            pltpu.VMEM((columns + 4, 8, BAND), f32),
            pltpu.VMEM((16 * columns, BAND), bf16),
        ],
        compiler_params=params(),
        name="depthwise_grad",
    )(
        index("space"), gate_grad, squeeze, reduce_t, excite_w, cell_rows, cells_t,
        expand_w, depth_w, half, grad_block, project_t, project_grad,
    )

    halves = packed.reshape(2, peers, share, broad)
    core = lax.axis_index("core")
    swap = [(0, 1), (1, 0)]
    keep = lax.dynamic_index_in_dim(halves, core, 0, False)
    send = lax.dynamic_index_in_dim(halves, 1 - core, 0, False)
    pieces = lax.all_to_all(
        keep + lax.ppermute(send, "core", swap), ("x", "y"), 0, 0, tiled=True
    )
    piece = jnp.sum(pieces, axis=0)
    for step in (1, 2):
        piece = piece + lax.ppermute(piece, "space", [(i, i ^ step) for i in range(space)])
    copies = jnp.broadcast_to(piece[None], pieces.shape)
    gathered = lax.all_to_all(copies, ("x", "y"), 0, 0, tiled=True)
    remote = lax.ppermute(gathered, "core", swap)
    return pl.pallas_call(
        unpack_kernel,
        in_specs=[SMEM] + [VMEM] * 2,
        out_specs=[VMEM] * 5,
        out_shape=[
            jax.ShapeDtypeStruct((1, channels, hidden), f32),
            jax.ShapeDtypeStruct((1, extent, extent, hidden), f32),
            jax.ShapeDtypeStruct((1, hidden, reduced), f32),
            jax.ShapeDtypeStruct((1, reduced, hidden), f32),
            jax.ShapeDtypeStruct((1, hidden, channels), f32),
        ],
        compiler_params=params(),
        name="unpack",
    )(index("core"), gathered.reshape(peers * share, broad), remote.reshape(peers * share, broad))


def solution(mesh):
    pipe, replica, space = (mesh.shape[name] for name in ("pipe", "replica", "space"))
    side = 1
    while 2 * side * side < replica:
        side *= 2
    fine = Mesh(
        mesh.devices.reshape(pipe, replica // (2 * side), side, 2, space),
        ("pipe", "x", "y", "core", "space"),
    )
    in_specs = (P("pipe", ("x", "y", "core"), "space"),) + (P("pipe"),) * 7
    return jax.shard_map(
        shards, mesh=fine, in_specs=in_specs, out_specs=(P("pipe"),) * 5, check_vma=False
    )
```

```python
import jax
import jax.numpy as jnp
from jax import lax
from jax.experimental import pallas as pl
from jax.experimental.pallas import tpu as pltpu
from jax.sharding import Mesh
from jax.sharding import PartitionSpec as P

loss_scale = 256.0
f32 = jnp.float32
bf16 = jnp.bfloat16
LANES = 128
BAND = 384
HEAD_CHUNK = 512
UNROLL = 2
STRIP = 50
WIDE = 100
TAPS = 50
VMEM = pl.BlockSpec(memory_space=pltpu.VMEM)
SMEM = pl.BlockSpec(memory_space=pltpu.SMEM)
ANY = pl.BlockSpec(memory_space=pl.ANY)
PARAMS = pltpu.CompilerParams(vmem_limit_bytes=60 * 1024 * 1024)


def up_to(size, multiple):
    return -(-size // multiple) * multiple


def started(*copies):
    made = [pltpu.make_async_copy(*copy) for copy in copies]
    for copy in made:
        copy.start()
    return made


def chunks(width, chunk, work):
    whole = width // chunk

    @pl.loop(0, whole, unroll=UNROLL)
    def each(part):
        work(pl.multiple_of(part * chunk, chunk), chunk)

    if width > whole * chunk:
        work(whole * chunk, width - whole * chunk)


def contract(left, right, left_dim, right_dim):
    return lax.dot_general(
        left, right, (((left_dim,), (right_dim,)), ((), ())), preferred_element_type=f32
    )


def row_window(own, rim, extent, place):
    margin = extent // 2
    window = []
    for i in range(extent):
        d = i - margin
        if d == 0:
            window.append(own)
        elif d > 0:
            window.append(pltpu.roll(jnp.where(place < d, rim, own), 8 - d, 0))
        else:
            window.append(pltpu.roll(jnp.where(place >= 8 + d, rim, own), -d, 0))
    return window


def forward_kernel(
    own_ref, before_ref, after_ref, expand_ref, depth_ref,
    cells_out, cells_t_out, mine_out, half_out, squeeze_ref,
    cells_ref, cells_t_ref, mine_ref, half_ref, left, right, expanded, sems,
):
    columns, channels = own_ref.shape[1:]
    extent, margin = 5, 2

    left[...] = jnp.zeros_like(left)
    right[...] = jnp.zeros_like(right)
    rest = channels - LANES
    for ref, base in ((own_ref, 0), (after_ref, 8), (before_ref, 14)):
        for y in range(ref.shape[0]):
            row = ref[y].astype(f32)
            left[pl.ds(base + y, columns, stride=16), :] = row[:, :LANES]
            right[pl.ds(base + y, columns, stride=16), :] = jnp.concatenate(
                [row[:, LANES:], jnp.zeros((columns, LANES - rest), f32)], axis=1
            )
    low, high = left[...], right[...]
    cells_ref[:, :LANES] = low.astype(bf16)
    cells_ref[:, LANES:] = high[:, :rest].astype(bf16)
    for start in range(0, 16 * columns, 320):
        cells_t_ref[:LANES, start : start + 320] = left[start : start + 320, :].T.astype(bf16)
        cells_t_ref[LANES:, start : start + 320] = right[start : start + 320, :].T[:rest].astype(
            bf16
        )
    mine_ref[:, :LANES] = (
        low.reshape(columns, 16, LANES)[:, :8].reshape(8 * columns, LANES).astype(bf16)
    )
    mine_ref[:, LANES:] = (
        high.reshape(columns, 16, LANES)[:, :8]
        .reshape(8 * columns, LANES)[:, :rest]
        .astype(bf16)
    )
    sends = started(
        (cells_ref, cells_out, sems.at[0]),
        (cells_t_ref, cells_t_out, sems.at[1]),
        (mine_ref, mine_out, sems.at[2]),
    )
    edge = jnp.zeros((margin, 16, expanded.shape[2]), f32)
    expanded[:margin] = edge
    expanded[margin + columns :] = edge

    @pl.loop(0, columns // WIDE)
    def expand(part):
        rows = pl.ds(pl.multiple_of(part * 16 * WIDE, 16 * WIDE), 16 * WIDE)
        half = jnp.dot(cells_ref[rows, :], expand_ref[...], preferred_element_type=f32)
        value = half + half * jnp.tanh(half)
        expanded[pl.ds(margin + part * WIDE, WIDE)] = value.reshape(WIDE, 16, half.shape[1])

    place = lax.broadcasted_iota(jnp.int32, (8, LANES), 0)

    @pl.loop(0, expanded.shape[2] // LANES)
    def convolve(tile):
        lanes = pl.ds(pl.multiple_of(tile * LANES, LANES), LANES)
        weight = [
            [depth_ref[i * extent + j : i * extent + j + 1, lanes] for j in range(extent)]
            for i in range(extent)
        ]

        def strip(number, total):
            x0 = number * STRIP
            sums = {}
            for k in range(STRIP + extent - 1):
                window = row_window(
                    expanded[x0 + k, :8, lanes], expanded[x0 + k, 8:, lanes], extent, place
                )
                for j in range(extent):
                    x = k - j
                    if 0 <= x < STRIP:
                        term = window[0] * weight[0][j]
                        for i in range(1, extent):
                            term = term + window[i] * weight[i][j]
                        sums[x] = term if x not in sums else sums[x] + term
                x = k - extent + 1
                if x >= 0:
                    half = 0.5 * sums.pop(x)
                    half_ref[pl.ds(pl.multiple_of((x0 + x) * 8, 8), 8), lanes] = half
                    total = total + (half + half * jnp.tanh(half))
            return total

        total = lax.fori_loop(0, columns // STRIP, strip, jnp.zeros((8, LANES), f32))
        squeeze_ref[:, lanes] = jnp.sum(total, axis=0, keepdims=True)
        pltpu.make_async_copy(
            half_ref.at[:, lanes], half_out.at[:, lanes], sems.at[3 + tile]
        ).start()

    for tile in range(half_ref.shape[1] // LANES):
        lanes = slice(tile * LANES, (tile + 1) * LANES)
        pltpu.make_async_copy(
            half_ref.at[:, lanes], half_out.at[:, lanes], sems.at[3 + tile]
        ).wait()
    for send in sends:
        send.wait()


def gate_of(squeeze, reduce_t, excite):
    reduced_in = jnp.sum(reduce_t * squeeze, axis=1, keepdims=True)
    reduced = reduced_in * jax.nn.sigmoid(reduced_in)
    gate = jax.nn.sigmoid(jnp.sum(excite * reduced, axis=0, keepdims=True))
    return reduced_in, reduced, gate


def head_kernel(
    half_in, squeeze_ref, reduce_ref, excite_ref, project_in, mine_in, head_in, class_in,
    logits_ref, gated_out, block_ref,
    half_ref, gated_ref, project_ref, mine_ref, head_ref, class_ref, gate_row, sums,
    sems, part_sems,
):
    cells = half_ref.shape[0]
    classes = class_ref.shape[0]

    def piece(part):
        rows = pl.ds(pl.multiple_of(part * 80, 80), 80)
        return half_in.at[rows, :], half_ref.at[rows, :], part_sems.at[part]

    for part in range(cells // 80):
        started(piece(part))
    project_copy, mine_copy, head_copy, class_copy = started(
        (project_in, project_ref, sems.at[3]),
        (mine_in, mine_ref, sems.at[4]),
        (head_in, head_ref, sems.at[0]),
        (class_in, class_ref, sems.at[1]),
    )
    cell_total = 4 * cells
    gate_row[...] = gate_of(squeeze_ref[...] / cell_total, reduce_ref[...], excite_ref[...])[2]

    @pl.loop(0, cells // 80)
    def gating(part):
        pltpu.make_async_copy(*piece(part)).wait()
        rows = pl.ds(pl.multiple_of(part * 80, 80), 80)
        half = half_ref[rows, :]
        gated_ref[rows, :] = ((half + half * jnp.tanh(half)) * gate_row[...]).astype(bf16)

    (send,) = started((gated_ref, gated_out, sems.at[2]))
    project_copy.wait()
    mine_copy.wait()
    residual = contract(gated_ref[...], project_ref[...], 1, 1)
    block = (mine_ref[...].astype(f32) + residual).astype(bf16)
    block_ref[...] = (0.5 * block.astype(f32)).astype(bf16)

    def head(first, count):
        lanes = pl.ds(first, count)
        half = jnp.dot(block_ref[...], head_ref[:, lanes], preferred_element_type=f32)
        act = half + half * jnp.tanh(half)
        sums[:, lanes] = jnp.sum(act.reshape(cells // 8, 8, count), axis=0)

    head_copy.wait()
    chunks(head_ref.shape[1], HEAD_CHUNK, head)
    class_copy.wait()
    pooled = sums[...]
    high = pooled.astype(bf16).astype(f32)
    both = jnp.concatenate([high, pooled - high], axis=0).astype(bf16)
    partial = jnp.sum(contract(both, class_ref[...], 1, 1), axis=0, keepdims=True)
    logits_ref[...] = jnp.zeros_like(logits_ref)
    logits_ref[:, :classes] = jnp.broadcast_to(
        partial / cell_total, (logits_ref.shape[0], classes)
    )
    send.wait()


def head_grad_kernel(
    which_ref, logits_ref, block_in, gated_in, project_in, head_in, class_in,
    grad_ref, project_grad_ref, gate_grad_ref,
    block_ref, gated_ref, project_ref, head_ref, class_ref, pooled, total, sems,
):
    class_copy, block_copy, head_copy, gated_copy, project_copy = started(
        (class_in, class_ref, sems.at[0]),
        (block_in, block_ref, sems.at[1]),
        (head_in, head_ref, sems.at[2]),
        (gated_in, gated_ref, sems.at[3]),
        (project_in, project_ref, sems.at[4]),
    )
    cells = block_ref.shape[0]
    classes = class_ref.shape[0]
    total[...] = jnp.zeros_like(total)

    rows = logits_ref[...]
    network = lax.broadcasted_iota(jnp.int32, rows.shape, 0) % 2
    valid = lax.broadcasted_iota(jnp.int32, (1, rows.shape[1]), 1) < classes
    teacher = jnp.sum(jnp.where(network == 0, rows, 0.0), axis=0, keepdims=True)
    student = jnp.sum(jnp.where(network == 1, rows, 0.0), axis=0, keepdims=True)
    exp_teacher = jnp.where(valid, jnp.exp(teacher), 0.0)
    prob = exp_teacher / jnp.sum(exp_teacher, axis=1, keepdims=True)
    log_sum = jnp.log(
        jnp.sum(jnp.where(valid, jnp.exp(student), 0.0), axis=1, keepdims=True)
    )
    logprob = student - log_sum
    cross = jnp.sum(prob * logprob, axis=1, keepdims=True)
    teacher_grad = loss_scale * prob * (cross - logprob)
    student_grad = loss_scale * (jnp.exp(logprob) - prob)
    grad = jnp.where(which_ref[0] == 0, teacher_grad, student_grad)
    grad = jnp.where(valid, grad, 0.0)
    grad = jnp.broadcast_to(grad, (16, rows.shape[1])).astype(bf16)[:, :classes]
    class_copy.wait()
    pooled[...] = contract(grad, class_ref[...], 1, 0)[:1] * (0.5 / (4 * cells))

    def head(first, count):
        lanes = pl.ds(first, count)
        weight = head_ref[:, lanes]
        half = jnp.dot(block_ref[...], weight, preferred_element_type=f32)
        t = jnp.tanh(half)
        slope = (1.0 + t) * (1.0 + (half - half * t))
        grad_head = (slope * pooled[:, lanes]).astype(bf16)
        total[...] += contract(grad_head, weight, 1, 1)

    block_copy.wait()
    head_copy.wait()
    chunks(head_ref.shape[1], HEAD_CHUNK, head)
    grad_block = total[...]
    grad_ref[...] = grad_block.astype(bf16)
    gated_copy.wait()
    project_copy.wait()
    project_grad = jnp.dot(grad_block.T.astype(bf16), gated_ref[...], preferred_element_type=f32)
    project_grad_ref[...] = project_grad
    gate_grad_ref[...] = jnp.sum(
        project_ref[...].astype(f32) * project_grad, axis=0, keepdims=True
    )


def backward_kernel(
    space_ref, gate_grad_ref, squeeze_ref, reduce_ref, excite_ref, cells_in, cells_t_in,
    expand_in, depth_ref, half_in, grad_in, project_in, project_grad_in,
    out_ref,
    cells_ref, cells_t_ref, expand_ref, half_ref, grad_ref, project_ref, gate_row, pool_row,
    expanded, slope, grad_depth, grad_expand, sems,
):
    channels = grad_in.shape[1]
    depth_base = 2 * channels
    arriving = started(
        (cells_in, cells_ref, sems.at[0]),
        (expand_in, expand_ref, sems.at[1]),
        (grad_in, grad_ref, sems.at[2]),
        (project_in, project_ref, sems.at[3]),
        (half_in, half_ref, sems.at[4]),
        (cells_t_in, cells_t_ref, sems.at[5]),
        (project_grad_in, out_ref.at[channels:depth_base, :], sems.at[6]),
    )
    cells = half_ref.shape[0]
    columns = cells // 8
    reduced_rows = reduce_ref.shape[0]
    extent, margin = 5, 2
    cell_total = 4 * cells
    excite_base = depth_base + up_to(extent * extent, 8)
    reduce_base = excite_base + reduced_rows
    end = reduce_base + reduced_rows

    squeeze = squeeze_ref[...] / cell_total
    reduced_in, reduced, gate = gate_of(squeeze, reduce_ref[...], excite_ref[...])
    grad_excite = (1.0 - gate) * gate_grad_ref[...]
    sigma = jax.nn.sigmoid(reduced_in)
    grad_reduced = jnp.sum(excite_ref[...] * grad_excite, axis=1, keepdims=True) * (
        sigma * (1.0 + reduced_in * (1.0 - sigma))
    )
    back_pool = jnp.sum(reduce_ref[...] * grad_reduced, axis=0, keepdims=True)
    gate_row[...] = 0.25 * gate
    pool_row[...] = back_pool * (0.25 / cell_total)
    once = jnp.where(space_ref[0] == 0, 1.0, 0.0)
    out_ref[excite_base:reduce_base, :] = reduced * (grad_excite * once)
    out_ref[reduce_base:end, :] = grad_reduced * (squeeze * once)
    if end < out_ref.shape[0]:
        out_ref[end:, :] = jnp.zeros((out_ref.shape[0] - end, out_ref.shape[1]), f32)
    edge = jnp.zeros((margin, 16, BAND), f32)
    expanded[:margin] = edge
    expanded[margin + columns :] = edge
    grad_depth[:margin] = edge[:, :8]
    grad_depth[margin + columns :] = edge[:, :8]

    for copy in arriving[:2]:
        copy.wait()

    @pl.loop(0, out_ref.shape[1] // BAND)
    def each(step):
        backward_band(
            step, arriving[2:], depth_base, excite_base,
            cells_ref, cells_t_ref, expand_ref, depth_ref, half_ref, grad_ref, project_ref,
            out_ref, gate_row, pool_row, expanded, slope, grad_depth, grad_expand,
        )


def backward_band(
    step, arriving, depth_base, excite_base,
    cells_ref, cells_t_ref, expand_ref, depth_ref, half_ref, grad_ref, project_ref,
    out_ref, gate_row, pool_row, expanded, slope, grad_depth, grad_expand,
):
    columns = half_ref.shape[0] // 8
    channels = grad_ref.shape[1]
    extent, margin = 5, 2
    start = pl.multiple_of(step * BAND, BAND)
    band = pl.ds(start, BAND)
    gate = gate_row[:, band]
    back_pool = pool_row[:, band]

    @pl.loop(0, columns // WIDE)
    def elements(part):
        rows = pl.ds(pl.multiple_of(part * 16 * WIDE, 16 * WIDE), 16 * WIDE)
        half = jnp.dot(cells_ref[rows, :], expand_ref[:, band], preferred_element_type=f32)
        t = jnp.tanh(half)
        turn = half * t
        expanded[pl.ds(margin + part * WIDE, WIDE)] = (half + turn).reshape(WIDE, 16, BAND)
        value = (1.0 + t) * (1.0 + (half - turn))
        slope[pl.ds(part * WIDE, WIDE)] = value.reshape(WIDE, 16, BAND)

    @pl.when(step == 0)
    def arrive():
        for copy in arriving:
            copy.wait()

    @pl.loop(0, columns // WIDE)
    def gradients(part):
        rows = pl.ds(pl.multiple_of(part * 8 * WIDE, 8 * WIDE), 8 * WIDE)
        grad_gated = jnp.dot(
            grad_ref[rows, :], project_ref[:, band], preferred_element_type=f32
        )
        half = half_ref[rows, band]
        t = jnp.tanh(half)
        value = (grad_gated * gate + back_pool) * ((1.0 + t) * (1.0 + (half - half * t)))
        grad_depth[pl.ds(margin + part * WIDE, WIDE)] = value.reshape(WIDE, 8, BAND)

    place = lax.broadcasted_iota(jnp.int32, (8, LANES), 0)

    @pl.loop(0, BAND // LANES)
    def convolve(tile):
        lanes = pl.ds(pl.multiple_of(tile * LANES, LANES), LANES)
        out_lanes = pl.ds(pl.multiple_of(start + tile * LANES, LANES), LANES)

        def taps(number, sums):
            sums = [list(line) for line in sums]
            base = margin + number * TAPS
            grads = {}
            for k in range(TAPS):
                window = row_window(
                    expanded[base + k, :8, lanes], expanded[base + k, 8:, lanes], extent, place
                )
                for j in range(extent):
                    place_x = k - j
                    if place_x not in grads:
                        grads[place_x] = grad_depth[base + place_x + margin, :, lanes]
                    for i in range(extent):
                        sums[i][j] = sums[i][j] + window[i] * grads[place_x]
            return tuple(tuple(line) for line in sums)

        zero = jnp.zeros((8, LANES), f32)
        sums = lax.fori_loop(0, columns // TAPS, taps, ((zero,) * extent,) * extent)
        for i in range(extent):
            for j in range(extent):
                row = depth_base + i * extent + j
                out_ref[row : row + 1, out_lanes] = 2.0 * jnp.sum(sums[i][j], axis=0, keepdims=True)
        for row in range(depth_base + extent * extent, excite_base):
            out_ref[row : row + 1, out_lanes] = jnp.zeros((1, LANES), f32)

        weight = [
            [depth_ref[i * extent + j : i * extent + j + 1, out_lanes] for j in range(extent)]
            for i in range(extent)
        ]

        @pl.loop(0, columns // STRIP)
        def spread(number):
            x0 = number * STRIP
            grads = [grad_depth[x0 + k, :, lanes] for k in range(extent - 1)]
            for x in range(STRIP):
                grads.append(grad_depth[x0 + x + extent - 1, :, lanes])
                whole, far = None, None
                for i in range(extent):
                    term = grads[x + extent - 1] * weight[i][0]
                    for j in range(1, extent):
                        term = term + grads[x + extent - 1 - j] * weight[i][j]
                    d = i - margin
                    if d != 0:
                        term = pltpu.roll(term, d % 8, 0)
                        inside = place >= d if d > 0 else place < 8 + d
                        leave = jnp.where(inside, 0.0, term)
                        far = leave if far is None else far + leave
                    whole = term if whole is None else whole + term
                near = whole - far
                near = near * slope[x0 + x, :8, lanes]
                far = far * slope[x0 + x, 8:, lanes]
                rows = pl.ds(pl.multiple_of((x0 + x) * 16, 16), 16)
                grad_expand[rows, lanes] = jnp.concatenate([near, far], axis=0).astype(bf16)

    out_ref[:channels, band] = jnp.dot(
        cells_t_ref[...], grad_expand[...], preferred_element_type=f32
    )


def unpack_kernel(
    core_ref, own_ref, other_ref, expand_ref, depth_ref, reduce_ref, excite_ref, project_ref
):
    channels, hidden = expand_ref.shape[1:]
    extent = depth_ref.shape[0]
    reduced = excite_ref.shape[0]
    depth_base = 2 * channels
    excite_base = depth_base + up_to(extent * extent, 8)
    reduce_base = excite_base + up_to(reduced, 8)
    half_rows = own_ref.shape[0]

    def rows(start, stop):
        pieces = []
        if start < half_rows:
            end = min(stop, half_rows)
            pieces.append(
                jnp.where(core_ref[0] == 0, own_ref[start:end, :], other_ref[start:end, :])
            )
        if stop > half_rows:
            begin = max(start, half_rows)
            pieces.append(
                jnp.where(
                    core_ref[0] == 0,
                    other_ref[begin - half_rows : stop - half_rows, :],
                    own_ref[begin - half_rows : stop - half_rows, :],
                )
            )
        return pieces[0] if len(pieces) == 1 else jnp.concatenate(pieces, axis=0)

    expand_ref[0] = rows(0, channels)[:, :hidden]
    project_ref[0] = rows(channels, depth_base)[:, :hidden]
    depth = rows(depth_base, excite_base)[:, :hidden]
    for i in range(extent):
        for j in range(extent):
            depth_ref[i, j] = depth[i * extent + j : i * extent + j + 1]
    excite = rows(excite_base, reduce_base)[:, :hidden]
    reduce = rows(reduce_base, reduce_base + up_to(reduced, 8))[:, :hidden]
    for row in range(reduced):
        excite_ref[row] = excite[row : row + 1]
        reduce_ref[row] = reduce[row : row + 1]


def shards(views, w_expand, w_depth, w_reduce, w_excite, w_project, w_head, w_class):
    own = views[0, 0]
    height, columns, channels = own.shape
    hidden = w_expand.shape[2]
    reduced = w_reduce.shape[2]
    extent = w_depth.shape[1]
    width = w_head.shape[2]
    classes = w_class.shape[2]
    cells = height * columns
    space = lax.axis_size("space")
    broad = up_to(hidden, BAND)
    tall = up_to(reduced, 8)

    up = [(i, i + 1) for i in range(space - 1)]
    down = [(i + 1, i) for i in range(space - 1)]
    before = lax.ppermute(own[height - 2 :], "space", up)
    after = lax.ppermute(own[:2], "space", down)

    fill = broad - hidden
    expand_w = jnp.pad(w_expand[0] * bf16(0.5), ((0, 0), (0, fill)))
    depth_w = jnp.pad(
        w_depth[0].reshape(extent * extent, hidden).astype(f32),
        ((0, up_to(extent * extent, 8) - extent * extent), (0, fill)),
    )
    reduce_t = jnp.pad(w_reduce[0].T.astype(f32), ((0, tall - reduced), (0, fill)))
    excite_w = jnp.pad(w_excite[0].astype(f32), ((0, tall - reduced), (0, fill)))
    class_t = w_class[0].T
    project_t = jnp.pad(w_project[0].T, ((0, 0), (0, fill)))

    depth_rows = depth_w.shape[0]
    cell_rows, cells_t, mine, half, squeeze = pl.pallas_call(
        forward_kernel,
        in_specs=[VMEM] * 5,
        out_specs=[ANY] * 4 + [VMEM],
        out_shape=[
            jax.ShapeDtypeStruct((16 * columns, channels), bf16),
            jax.ShapeDtypeStruct((channels, 16 * columns), bf16),
            jax.ShapeDtypeStruct((cells, channels), bf16),
            jax.ShapeDtypeStruct((cells, broad), f32),
            jax.ShapeDtypeStruct((1, broad), f32),
        ],
        scratch_shapes=[
            pltpu.VMEM((16 * columns, channels), bf16),
            pltpu.VMEM((channels, 16 * columns), bf16),
            pltpu.VMEM((cells, channels), bf16),
            pltpu.VMEM((cells, broad), f32),
            pltpu.VMEM((16 * columns, LANES), f32),
            pltpu.VMEM((16 * columns, LANES), f32),
            pltpu.VMEM((columns + 4, 16, broad), f32),
            pltpu.SemaphoreType.DMA((3 + broad // LANES,)),
        ],
        compiler_params=PARAMS,
        name="expand_depthwise",
    )(own, before, after, expand_w, depth_w)
    squeeze = lax.psum(squeeze, "space")

    ranks = 2 * space
    logits, gated, block = pl.pallas_call(
        head_kernel,
        in_specs=[ANY] + [VMEM] * 3 + [ANY] * 4,
        out_specs=[VMEM, ANY, VMEM],
        out_shape=[
            jax.ShapeDtypeStruct((ranks, up_to(classes, LANES)), f32),
            jax.ShapeDtypeStruct((cells, broad), bf16),
            jax.ShapeDtypeStruct((cells, channels), bf16),
        ],
        scratch_shapes=[
            pltpu.VMEM((cells, broad), f32),
            pltpu.VMEM((cells, broad), bf16),
            pltpu.VMEM((channels, broad), bf16),
            pltpu.VMEM((cells, channels), bf16),
            pltpu.VMEM((channels, width), bf16),
            pltpu.VMEM((classes, width), bf16),
            pltpu.VMEM((1, broad), f32),
            pltpu.VMEM((8, width), f32),
            pltpu.SemaphoreType.DMA((5,)),
            pltpu.SemaphoreType.DMA((cells // 80,)),
        ],
        compiler_params=PARAMS,
        name="project_head",
    )(half, squeeze, reduce_t, excite_w, project_t, mine, w_head[0], class_t)
    logits = lax.all_to_all(logits, ("space", "pipe"), 0, 0, tiled=True)

    def index(name):
        return lax.axis_index(name).astype(jnp.int32).reshape(1)

    grad_block, project_grad, gate_grad = pl.pallas_call(
        head_grad_kernel,
        in_specs=[SMEM, VMEM] + [ANY] * 5,
        out_specs=[VMEM] * 3,
        out_shape=[
            jax.ShapeDtypeStruct((cells, channels), bf16),
            jax.ShapeDtypeStruct((channels, broad), f32),
            jax.ShapeDtypeStruct((1, broad), f32),
        ],
        scratch_shapes=[
            pltpu.VMEM((cells, channels), bf16),
            pltpu.VMEM((cells, broad), bf16),
            pltpu.VMEM((channels, broad), bf16),
            pltpu.VMEM((channels, width), bf16),
            pltpu.VMEM((classes, width), bf16),
            pltpu.VMEM((1, width), f32),
            pltpu.VMEM((cells, channels), f32),
            pltpu.SemaphoreType.DMA((5,)),
        ],
        compiler_params=PARAMS,
        name="head_grad",
    )(index("pipe"), logits, block, gated, project_t, w_head[0], class_t)
    gate_grad = lax.psum(gate_grad, "space")

    peers = lax.axis_size("x") * lax.axis_size("y")
    used = 2 * channels + depth_rows + 2 * tall
    share = up_to(-(-used // (2 * peers)), 8)
    rows = 2 * peers * share
    packed = pl.pallas_call(
        backward_kernel,
        in_specs=[SMEM] + [VMEM] * 4 + [ANY] * 3 + [VMEM] + [ANY] * 4,
        out_specs=VMEM,
        out_shape=jax.ShapeDtypeStruct((rows, broad), f32),
        scratch_shapes=[
            pltpu.VMEM((16 * columns, channels), bf16),
            pltpu.VMEM((channels, 16 * columns), bf16),
            pltpu.VMEM((channels, broad), bf16),
            pltpu.VMEM((cells, broad), f32),
            pltpu.VMEM((cells, channels), bf16),
            pltpu.VMEM((channels, broad), bf16),
            pltpu.VMEM((1, broad), f32),
            pltpu.VMEM((1, broad), f32),
            pltpu.VMEM((columns + 4, 16, BAND), f32),
            pltpu.VMEM((columns, 16, BAND), f32),
            pltpu.VMEM((columns + 4, 8, BAND), f32),
            pltpu.VMEM((16 * columns, BAND), bf16),
            pltpu.SemaphoreType.DMA((7,)),
        ],
        compiler_params=PARAMS,
        name="depthwise_grad",
    )(
        index("space"), gate_grad, squeeze, reduce_t, excite_w, cell_rows, cells_t,
        expand_w, depth_w, half, grad_block, project_t, project_grad,
    )

    halves = packed.reshape(2, peers, share, broad)
    core = lax.axis_index("core")
    swap = [(0, 1), (1, 0)]
    keep = lax.dynamic_index_in_dim(halves, core, 0, False)
    send = lax.dynamic_index_in_dim(halves, 1 - core, 0, False)
    pieces = lax.all_to_all(
        keep + lax.ppermute(send, "core", swap), ("x", "y"), 0, 0, tiled=True
    )
    piece = jnp.sum(pieces, axis=0)
    for step in (1, 2):
        piece = piece + lax.ppermute(piece, "space", [(i, i ^ step) for i in range(space)])
    copies = jnp.broadcast_to(piece[None], pieces.shape)
    gathered = lax.all_to_all(copies, ("x", "y"), 0, 0, tiled=True)
    remote = lax.ppermute(gathered, "core", swap)
    g_expand, g_depth, g_reduce, g_excite, g_project = pl.pallas_call(
        unpack_kernel,
        in_specs=[SMEM] + [VMEM] * 2,
        out_specs=[VMEM] * 5,
        out_shape=[
            jax.ShapeDtypeStruct((1, channels, hidden), f32),
            jax.ShapeDtypeStruct((extent, extent, 1, hidden), f32),
            jax.ShapeDtypeStruct((reduced, 1, hidden), f32),
            jax.ShapeDtypeStruct((reduced, 1, hidden), f32),
            jax.ShapeDtypeStruct((1, channels, hidden), f32),
        ],
        compiler_params=PARAMS,
        name="unpack",
    )(index("core"), gathered.reshape(peers * share, broad), remote.reshape(peers * share, broad))
    return (
        g_expand,
        g_depth.transpose(2, 0, 1, 3),
        g_reduce.transpose(1, 2, 0),
        g_excite.transpose(1, 0, 2),
        g_project.transpose(0, 2, 1),
    )


def solution(mesh):
    pipe, replica, space = (mesh.shape[name] for name in ("pipe", "replica", "space"))
    side = 1
    while 2 * side * side < replica:
        side *= 2
    fine = Mesh(
        mesh.devices.reshape(pipe, replica // (2 * side), side, 2, space),
        ("pipe", "x", "y", "core", "space"),
    )
    in_specs = (P("pipe", ("x", "y", "core"), "space"),) + (P("pipe"),) * 7
    return jax.shard_map(
        shards, mesh=fine, in_specs=in_specs, out_specs=(P("pipe"),) * 5, check_vma=False
    )
```

```python
import jax
import jax.numpy as jnp
from jax import lax
from jax.experimental import pallas as pl
from jax.experimental.pallas import tpu as pltpu
from jax.sharding import Mesh
from jax.sharding import PartitionSpec as P

loss_scale = 256.0
f32 = jnp.float32
bf16 = jnp.bfloat16
LANES = 128
BAND = 384
HEAD_CHUNK = 512
STRIP = 50
WIDE = 100
TAPS = 50
VMEM = pl.BlockSpec(memory_space=pltpu.VMEM)
SMEM = pl.BlockSpec(memory_space=pltpu.SMEM)
ANY = pl.BlockSpec(memory_space=pl.ANY)
PARAMS = pltpu.CompilerParams(vmem_limit_bytes=60 * 1024 * 1024)


def up_to(size, multiple):
    return -(-size // multiple) * multiple


def started(*copies):
    made = [pltpu.make_async_copy(*copy) for copy in copies]
    for copy in made:
        copy.start()
    return made


def chunks(width, chunk, unroll, work):
    whole = width // chunk

    @pl.loop(0, whole, unroll=unroll)
    def each(part):
        work(pl.multiple_of(part * chunk, chunk), chunk)

    if width > whole * chunk:
        work(whole * chunk, width - whole * chunk)


def contract(left, right, left_dim, right_dim):
    return lax.dot_general(
        left, right, (((left_dim,), (right_dim,)), ((), ())), preferred_element_type=f32
    )


def row_window(own, rim, extent, place):
    margin = extent // 2
    window = []
    for i in range(extent):
        d = i - margin
        if d == 0:
            window.append(own)
        elif d > 0:
            window.append(pltpu.roll(jnp.where(place < d, rim, own), 8 - d, 0))
        else:
            window.append(pltpu.roll(jnp.where(place >= 8 + d, rim, own), -d, 0))
    return window


def forward_kernel(
    own_ref, before_ref, after_ref, expand_ref, depth_ref,
    cells_out, cells_t_out, mine_out, half_out, squeeze_ref,
    cells_ref, cells_t_ref, mine_ref, half_ref, left, right, expanded, sems,
):
    columns, channels = own_ref.shape[1:]
    extent, margin = 5, 2

    left[...] = jnp.zeros_like(left)
    right[...] = jnp.zeros_like(right)
    rest = channels - LANES
    for ref, base in ((own_ref, 0), (after_ref, 8), (before_ref, 14)):
        for y in range(ref.shape[0]):
            row = ref[y].astype(f32)
            left[pl.ds(base + y, columns, stride=16), :] = row[:, :LANES]
            right[pl.ds(base + y, columns, stride=16), :] = jnp.concatenate(
                [row[:, LANES:], jnp.zeros((columns, LANES - rest), f32)], axis=1
            )
    low, high = left[...], right[...]
    cells_ref[:, :LANES] = low.astype(bf16)
    cells_ref[:, LANES:] = high[:, :rest].astype(bf16)
    for start in range(0, 16 * columns, 320):
        cells_t_ref[:LANES, start : start + 320] = left[start : start + 320, :].T.astype(bf16)
        cells_t_ref[LANES:, start : start + 320] = right[start : start + 320, :].T[:rest].astype(
            bf16
        )
    mine_ref[:, :LANES] = (
        low.reshape(columns, 16, LANES)[:, :8].reshape(8 * columns, LANES).astype(bf16)
    )
    mine_ref[:, LANES:] = (
        high.reshape(columns, 16, LANES)[:, :8]
        .reshape(8 * columns, LANES)[:, :rest]
        .astype(bf16)
    )
    sends = started(
        (cells_ref, cells_out, sems.at[0]),
        (cells_t_ref, cells_t_out, sems.at[1]),
        (mine_ref, mine_out, sems.at[2]),
    )
    edge = jnp.zeros((margin, 16, expanded.shape[2]), f32)
    expanded[:margin] = edge
    expanded[margin + columns :] = edge

    @pl.loop(0, columns // WIDE)
    def expand(part):
        rows = pl.ds(pl.multiple_of(part * 16 * WIDE, 16 * WIDE), 16 * WIDE)
        half = jnp.dot(cells_ref[rows, :], expand_ref[...], preferred_element_type=f32)
        value = half + half * jnp.tanh(half)
        expanded[pl.ds(margin + part * WIDE, WIDE)] = value.reshape(WIDE, 16, half.shape[1])

    place = lax.broadcasted_iota(jnp.int32, (8, LANES), 0)

    @pl.loop(0, expanded.shape[2] // LANES)
    def convolve(tile):
        lanes = pl.ds(pl.multiple_of(tile * LANES, LANES), LANES)
        weight = [
            [depth_ref[i * extent + j : i * extent + j + 1, lanes] for j in range(extent)]
            for i in range(extent)
        ]

        def strip(number, total):
            x0 = number * STRIP
            sums = {}
            for k in range(STRIP + extent - 1):
                window = row_window(
                    expanded[x0 + k, :8, lanes], expanded[x0 + k, 8:, lanes], extent, place
                )
                for j in range(extent):
                    x = k - j
                    if 0 <= x < STRIP:
                        term = window[0] * weight[0][j]
                        for i in range(1, extent):
                            term = term + window[i] * weight[i][j]
                        sums[x] = term if x not in sums else sums[x] + term
                x = k - extent + 1
                if x >= 0:
                    half = 0.5 * sums.pop(x)
                    half_ref[pl.ds(pl.multiple_of((x0 + x) * 8, 8), 8), lanes] = half
                    total = total + (half + half * jnp.tanh(half))
            return total

        total = lax.fori_loop(0, columns // STRIP, strip, jnp.zeros((8, LANES), f32))
        squeeze_ref[:, lanes] = jnp.sum(total, axis=0, keepdims=True)
        pltpu.make_async_copy(
            half_ref.at[:, lanes], half_out.at[:, lanes], sems.at[3 + tile]
        ).start()

    for tile in range(half_ref.shape[1] // LANES):
        lanes = slice(tile * LANES, (tile + 1) * LANES)
        pltpu.make_async_copy(
            half_ref.at[:, lanes], half_out.at[:, lanes], sems.at[3 + tile]
        ).wait()
    for send in sends:
        send.wait()


def gate_of(squeeze, reduce_t, excite):
    reduced_in = jnp.sum(reduce_t * squeeze, axis=1, keepdims=True)
    reduced = reduced_in * jax.nn.sigmoid(reduced_in)
    gate = jax.nn.sigmoid(jnp.sum(excite * reduced, axis=0, keepdims=True))
    return reduced_in, reduced, gate


def head_kernel(
    half_in, squeeze_ref, reduce_ref, excite_ref, project_in, mine_in, head_in, class_in,
    logits_ref, gated_out, block_ref,
    half_ref, gated_ref, project_ref, mine_ref, head_ref, class_ref, gate_row, sums,
    sems, part_sems,
):
    cells = half_ref.shape[0]
    classes = class_ref.shape[0]

    def piece(part):
        rows = pl.ds(pl.multiple_of(part * 80, 80), 80)
        return half_in.at[rows, :], half_ref.at[rows, :], part_sems.at[part]

    for part in range(cells // 80):
        started(piece(part))
    project_copy, mine_copy, head_copy, class_copy = started(
        (project_in, project_ref, sems.at[3]),
        (mine_in, mine_ref, sems.at[4]),
        (head_in, head_ref, sems.at[0]),
        (class_in, class_ref, sems.at[1]),
    )
    cell_total = 4 * cells
    gate_row[...] = gate_of(squeeze_ref[...] / cell_total, reduce_ref[...], excite_ref[...])[2]

    @pl.loop(0, cells // 80)
    def gating(part):
        pltpu.make_async_copy(*piece(part)).wait()
        rows = pl.ds(pl.multiple_of(part * 80, 80), 80)
        half = half_ref[rows, :]
        gated_ref[rows, :] = ((half + half * jnp.tanh(half)) * gate_row[...]).astype(bf16)

    (send,) = started((gated_ref, gated_out, sems.at[2]))
    project_copy.wait()
    mine_copy.wait()
    residual = contract(gated_ref[...], project_ref[...], 1, 1)
    block = (mine_ref[...].astype(f32) + residual).astype(bf16)
    block_ref[...] = (0.5 * block.astype(f32)).astype(bf16)

    def head(first, count):
        lanes = pl.ds(first, count)
        half = jnp.dot(block_ref[...], head_ref[:, lanes], preferred_element_type=f32)
        act = half + half * jnp.tanh(half)
        sums[:, lanes] = jnp.sum(act.reshape(cells // 8, 8, count), axis=0)

    head_copy.wait()
    chunks(head_ref.shape[1], HEAD_CHUNK, 5, head)
    class_copy.wait()
    pooled = sums[...]
    high = pooled.astype(bf16).astype(f32)
    both = jnp.concatenate([high, pooled - high], axis=0).astype(bf16)
    partial = jnp.sum(contract(both, class_ref[...], 1, 1), axis=0, keepdims=True)
    logits_ref[...] = jnp.zeros_like(logits_ref)
    for rank in range(logits_ref.shape[0]):
        logits_ref[rank, :, :classes] = partial / cell_total
    send.wait()


def head_grad_kernel(
    which_ref, logits_ref, block_in, gated_in, project_in, head_in, class_in,
    grad_ref, project_grad_ref, gate_grad_ref,
    block_ref, gated_ref, project_ref, head_ref, class_ref, pooled, total, sems,
):
    class_copy, block_copy, head_copy, gated_copy, project_copy = started(
        (class_in, class_ref, sems.at[0]),
        (block_in, block_ref, sems.at[1]),
        (head_in, head_ref, sems.at[2]),
        (gated_in, gated_ref, sems.at[3]),
        (project_in, project_ref, sems.at[4]),
    )
    cells = block_ref.shape[0]
    classes = class_ref.shape[0]
    total[...] = jnp.zeros_like(total)

    ranks, wide = logits_ref.shape[0], logits_ref.shape[2]
    valid = lax.broadcasted_iota(jnp.int32, (1, wide), 1) < classes
    teacher, student = logits_ref[0], logits_ref[1]
    for rank in range(2, ranks, 2):
        teacher = teacher + logits_ref[rank]
        student = student + logits_ref[rank + 1]
    exp_teacher = jnp.where(valid, jnp.exp(teacher), 0.0)
    prob = exp_teacher / jnp.sum(exp_teacher, axis=1, keepdims=True)
    log_sum = jnp.log(
        jnp.sum(jnp.where(valid, jnp.exp(student), 0.0), axis=1, keepdims=True)
    )
    logprob = student - log_sum
    cross = jnp.sum(prob * logprob, axis=1, keepdims=True)
    teacher_grad = loss_scale * prob * (cross - logprob)
    student_grad = loss_scale * (jnp.exp(logprob) - prob)
    grad = jnp.where(which_ref[0] == 0, teacher_grad, student_grad)
    grad = jnp.where(valid, grad, 0.0)
    grad = jnp.broadcast_to(grad, (16, wide)).astype(bf16)[:, :classes]
    class_copy.wait()
    pooled[...] = contract(grad, class_ref[...], 1, 0)[:1] * (0.5 / (4 * cells))

    def head(first, count):
        lanes = pl.ds(first, count)
        weight = head_ref[:, lanes]
        half = jnp.dot(block_ref[...], weight, preferred_element_type=f32)
        t = jnp.tanh(half)
        slope = (1.0 + t) * (1.0 + (half - half * t))
        grad_head = (slope * pooled[:, lanes]).astype(bf16)
        total[...] += contract(grad_head, weight, 1, 1)

    block_copy.wait()
    head_copy.wait()
    chunks(head_ref.shape[1], HEAD_CHUNK, 10, head)
    grad_block = total[...]
    grad_ref[...] = grad_block.astype(bf16)
    gated_copy.wait()
    project_copy.wait()
    project_grad = jnp.dot(grad_block.T.astype(bf16), gated_ref[...], preferred_element_type=f32)
    project_grad_ref[...] = project_grad
    gate_grad_ref[...] = jnp.sum(
        project_ref[...].astype(f32) * project_grad, axis=0, keepdims=True
    )


def backward_kernel(
    space_ref, gate_grad_ref, squeeze_ref, reduce_ref, excite_ref, cells_in, cells_t_in,
    expand_in, depth_ref, half_in, grad_in, project_in, project_grad_in,
    out_ref,
    cells_ref, cells_t_ref, expand_ref, half_ref, grad_ref, project_ref, gate_row, pool_row,
    expanded, slope, grad_depth, grad_expand, sems,
):
    channels = grad_in.shape[1]
    depth_base = 2 * channels
    arriving = started(
        (cells_in, cells_ref, sems.at[0]),
        (expand_in, expand_ref, sems.at[1]),
        (grad_in, grad_ref, sems.at[2]),
        (project_in, project_ref, sems.at[3]),
        (half_in, half_ref, sems.at[4]),
        (cells_t_in, cells_t_ref, sems.at[5]),
        (project_grad_in, out_ref.at[channels:depth_base, :], sems.at[6]),
    )
    cells = half_ref.shape[0]
    columns = cells // 8
    reduced_rows = reduce_ref.shape[0]
    extent, margin = 5, 2
    cell_total = 4 * cells
    excite_base = depth_base + up_to(extent * extent, 8)
    reduce_base = excite_base + reduced_rows
    end = reduce_base + reduced_rows

    squeeze = squeeze_ref[...] / cell_total
    reduced_in, reduced, gate = gate_of(squeeze, reduce_ref[...], excite_ref[...])
    grad_excite = (1.0 - gate) * gate_grad_ref[...]
    sigma = jax.nn.sigmoid(reduced_in)
    grad_reduced = jnp.sum(excite_ref[...] * grad_excite, axis=1, keepdims=True) * (
        sigma * (1.0 + reduced_in * (1.0 - sigma))
    )
    back_pool = jnp.sum(reduce_ref[...] * grad_reduced, axis=0, keepdims=True)
    gate_row[...] = 0.25 * gate
    pool_row[...] = back_pool * (0.25 / cell_total)
    once = jnp.where(space_ref[0] == 0, 1.0, 0.0)
    out_ref[excite_base:reduce_base, :] = reduced * (grad_excite * once)
    out_ref[reduce_base:end, :] = grad_reduced * (squeeze * once)
    if end < out_ref.shape[0]:
        out_ref[end:, :] = jnp.zeros((out_ref.shape[0] - end, out_ref.shape[1]), f32)
    edge = jnp.zeros((margin, 16, BAND), f32)
    expanded[:margin] = edge
    expanded[margin + columns :] = edge
    grad_depth[:margin] = edge[:, :8]
    grad_depth[margin + columns :] = edge[:, :8]

    for copy in arriving[:2]:
        copy.wait()

    @pl.loop(0, out_ref.shape[1] // BAND)
    def each(step):
        backward_band(
            step, arriving[2:], depth_base, excite_base,
            cells_ref, cells_t_ref, expand_ref, depth_ref, half_ref, grad_ref, project_ref,
            out_ref, gate_row, pool_row, expanded, slope, grad_depth, grad_expand,
        )


def backward_band(
    step, arriving, depth_base, excite_base,
    cells_ref, cells_t_ref, expand_ref, depth_ref, half_ref, grad_ref, project_ref,
    out_ref, gate_row, pool_row, expanded, slope, grad_depth, grad_expand,
):
    columns = half_ref.shape[0] // 8
    channels = grad_ref.shape[1]
    extent, margin = 5, 2
    start = pl.multiple_of(step * BAND, BAND)
    band = pl.ds(start, BAND)
    gate = gate_row[:, band]
    back_pool = pool_row[:, band]

    @pl.loop(0, columns // WIDE)
    def elements(part):
        rows = pl.ds(pl.multiple_of(part * 16 * WIDE, 16 * WIDE), 16 * WIDE)
        half = jnp.dot(cells_ref[rows, :], expand_ref[:, band], preferred_element_type=f32)
        t = jnp.tanh(half)
        turn = half * t
        expanded[pl.ds(margin + part * WIDE, WIDE)] = (half + turn).reshape(WIDE, 16, BAND)
        value = (1.0 + t) * (1.0 + (half - turn))
        slope[pl.ds(part * WIDE, WIDE)] = value.reshape(WIDE, 16, BAND)

    @pl.when(step == 0)
    def arrive():
        for copy in arriving:
            copy.wait()

    @pl.loop(0, columns // WIDE)
    def gradients(part):
        rows = pl.ds(pl.multiple_of(part * 8 * WIDE, 8 * WIDE), 8 * WIDE)
        grad_gated = jnp.dot(
            grad_ref[rows, :], project_ref[:, band], preferred_element_type=f32
        )
        half = half_ref[rows, band]
        t = jnp.tanh(half)
        value = (grad_gated * gate + back_pool) * ((1.0 + t) * (1.0 + (half - half * t)))
        grad_depth[pl.ds(margin + part * WIDE, WIDE)] = value.reshape(WIDE, 8, BAND)

    place = lax.broadcasted_iota(jnp.int32, (8, LANES), 0)

    @pl.loop(0, BAND // LANES)
    def convolve(tile):
        lanes = pl.ds(pl.multiple_of(tile * LANES, LANES), LANES)
        out_lanes = pl.ds(pl.multiple_of(start + tile * LANES, LANES), LANES)

        def taps(number, sums):
            sums = [list(line) for line in sums]
            base = margin + number * TAPS
            grads = {}
            for k in range(TAPS):
                window = row_window(
                    expanded[base + k, :8, lanes], expanded[base + k, 8:, lanes], extent, place
                )
                for j in range(extent):
                    place_x = k - j
                    if place_x not in grads:
                        grads[place_x] = grad_depth[base + place_x + margin, :, lanes]
                    for i in range(extent):
                        sums[i][j] = sums[i][j] + window[i] * grads[place_x]
            return tuple(tuple(line) for line in sums)

        zero = jnp.zeros((8, LANES), f32)
        sums = lax.fori_loop(0, columns // TAPS, taps, ((zero,) * extent,) * extent)
        for i in range(extent):
            for j in range(extent):
                row = depth_base + i * extent + j
                out_ref[row : row + 1, out_lanes] = 2.0 * jnp.sum(sums[i][j], axis=0, keepdims=True)
        for row in range(depth_base + extent * extent, excite_base):
            out_ref[row : row + 1, out_lanes] = jnp.zeros((1, LANES), f32)

        weight = [
            [depth_ref[i * extent + j : i * extent + j + 1, out_lanes] for j in range(extent)]
            for i in range(extent)
        ]

        @pl.loop(0, columns // STRIP)
        def spread(number):
            x0 = number * STRIP
            grads = [grad_depth[x0 + k, :, lanes] for k in range(extent - 1)]
            for x in range(STRIP):
                grads.append(grad_depth[x0 + x + extent - 1, :, lanes])
                whole, far = None, None
                for i in range(extent):
                    term = grads[x + extent - 1] * weight[i][0]
                    for j in range(1, extent):
                        term = term + grads[x + extent - 1 - j] * weight[i][j]
                    d = i - margin
                    if d != 0:
                        term = pltpu.roll(term, d % 8, 0)
                        inside = place >= d if d > 0 else place < 8 + d
                        leave = jnp.where(inside, 0.0, term)
                        far = leave if far is None else far + leave
                    whole = term if whole is None else whole + term
                near = whole - far
                near = near * slope[x0 + x, :8, lanes]
                far = far * slope[x0 + x, 8:, lanes]
                rows = pl.ds(pl.multiple_of((x0 + x) * 16, 16), 16)
                grad_expand[rows, lanes] = jnp.concatenate([near, far], axis=0).astype(bf16)

    out_ref[:channels, band] = jnp.dot(
        cells_t_ref[...], grad_expand[...], preferred_element_type=f32
    )


def unpack_kernel(
    core_ref, own_ref, other_ref, expand_ref, depth_ref, reduce_ref, excite_ref, project_ref
):
    channels, hidden = expand_ref.shape[1:]
    extent = depth_ref.shape[0]
    reduced = excite_ref.shape[0]
    depth_base = 2 * channels
    excite_base = depth_base + up_to(extent * extent, 8)
    reduce_base = excite_base + up_to(reduced, 8)
    half_rows = own_ref.shape[0]

    def rows(start, stop):
        pieces = []
        if start < half_rows:
            end = min(stop, half_rows)
            pieces.append(
                jnp.where(
                    core_ref[0] == 0,
                    own_ref[start:end, :].astype(f32),
                    other_ref[start:end, :].astype(f32),
                )
            )
        if stop > half_rows:
            begin = max(start, half_rows)
            pieces.append(
                jnp.where(
                    core_ref[0] == 0,
                    other_ref[begin - half_rows : stop - half_rows, :].astype(f32),
                    own_ref[begin - half_rows : stop - half_rows, :].astype(f32),
                )
            )
        return pieces[0] if len(pieces) == 1 else jnp.concatenate(pieces, axis=0)

    expand_ref[0] = rows(0, channels)[:, :hidden]
    project_ref[0] = rows(channels, depth_base)[:, :hidden]
    depth = rows(depth_base, excite_base)[:, :hidden]
    for i in range(extent):
        for j in range(extent):
            depth_ref[i, j] = depth[i * extent + j : i * extent + j + 1]
    excite = rows(excite_base, reduce_base)[:, :hidden]
    reduce = rows(reduce_base, reduce_base + up_to(reduced, 8))[:, :hidden]
    for row in range(reduced):
        excite_ref[row] = excite[row : row + 1]
        reduce_ref[row] = reduce[row : row + 1]


def shards(views, w_expand, w_depth, w_reduce, w_excite, w_project, w_head, w_class):
    own = views[0, 0]
    height, columns, channels = own.shape
    hidden = w_expand.shape[2]
    reduced = w_reduce.shape[2]
    extent = w_depth.shape[1]
    width = w_head.shape[2]
    classes = w_class.shape[2]
    cells = height * columns
    space = lax.axis_size("space")
    broad = up_to(hidden, BAND)
    tall = up_to(reduced, 8)

    up = [(i, i + 1) for i in range(space - 1)]
    down = [(i + 1, i) for i in range(space - 1)]
    before = lax.ppermute(own[height - 2 :], "space", up)
    after = lax.ppermute(own[:2], "space", down)

    fill = broad - hidden
    expand_w = jnp.pad(w_expand[0] * bf16(0.5), ((0, 0), (0, fill)))
    depth_w = jnp.pad(
        w_depth[0].reshape(extent * extent, hidden).astype(f32),
        ((0, up_to(extent * extent, 8) - extent * extent), (0, fill)),
    )
    reduce_t = jnp.pad(w_reduce[0].T.astype(f32), ((0, tall - reduced), (0, fill)))
    excite_w = jnp.pad(w_excite[0].astype(f32), ((0, tall - reduced), (0, fill)))
    class_t = w_class[0].T
    project_t = jnp.pad(w_project[0].T, ((0, 0), (0, fill)))

    depth_rows = depth_w.shape[0]
    cell_rows, cells_t, mine, half, squeeze = pl.pallas_call(
        forward_kernel,
        in_specs=[VMEM] * 5,
        out_specs=[ANY] * 4 + [VMEM],
        out_shape=[
            jax.ShapeDtypeStruct((16 * columns, channels), bf16),
            jax.ShapeDtypeStruct((channels, 16 * columns), bf16),
            jax.ShapeDtypeStruct((cells, channels), bf16),
            jax.ShapeDtypeStruct((cells, broad), f32),
            jax.ShapeDtypeStruct((1, broad), f32),
        ],
        scratch_shapes=[
            pltpu.VMEM((16 * columns, channels), bf16),
            pltpu.VMEM((channels, 16 * columns), bf16),
            pltpu.VMEM((cells, channels), bf16),
            pltpu.VMEM((cells, broad), f32),
            pltpu.VMEM((16 * columns, LANES), f32),
            pltpu.VMEM((16 * columns, LANES), f32),
            pltpu.VMEM((columns + 4, 16, broad), f32),
            pltpu.SemaphoreType.DMA((3 + broad // LANES,)),
        ],
        compiler_params=PARAMS,
        name="expand_depthwise",
    )(own, before, after, expand_w, depth_w)
    squeeze = lax.psum(squeeze, "space")

    ranks = 2 * space
    logits, gated, block = pl.pallas_call(
        head_kernel,
        in_specs=[ANY] + [VMEM] * 3 + [ANY] * 4,
        out_specs=[VMEM, ANY, VMEM],
        out_shape=[
            jax.ShapeDtypeStruct((ranks, 1, up_to(classes, LANES)), f32),
            jax.ShapeDtypeStruct((cells, broad), bf16),
            jax.ShapeDtypeStruct((cells, channels), bf16),
        ],
        scratch_shapes=[
            pltpu.VMEM((cells, broad), f32),
            pltpu.VMEM((cells, broad), bf16),
            pltpu.VMEM((channels, broad), bf16),
            pltpu.VMEM((cells, channels), bf16),
            pltpu.VMEM((channels, width), bf16),
            pltpu.VMEM((classes, width), bf16),
            pltpu.VMEM((1, broad), f32),
            pltpu.VMEM((8, width), f32),
            pltpu.SemaphoreType.DMA((5,)),
            pltpu.SemaphoreType.DMA((cells // 80,)),
        ],
        compiler_params=PARAMS,
        name="project_head",
    )(half, squeeze, reduce_t, excite_w, project_t, mine, w_head[0], class_t)
    logits = lax.all_to_all(logits, ("space", "pipe"), 0, 0, tiled=True)

    def index(name):
        return lax.axis_index(name).astype(jnp.int32).reshape(1)

    grad_block, project_grad, gate_grad = pl.pallas_call(
        head_grad_kernel,
        in_specs=[SMEM, VMEM] + [ANY] * 5,
        out_specs=[VMEM] * 3,
        out_shape=[
            jax.ShapeDtypeStruct((cells, channels), bf16),
            jax.ShapeDtypeStruct((channels, broad), f32),
            jax.ShapeDtypeStruct((1, broad), f32),
        ],
        scratch_shapes=[
            pltpu.VMEM((cells, channels), bf16),
            pltpu.VMEM((cells, broad), bf16),
            pltpu.VMEM((channels, broad), bf16),
            pltpu.VMEM((channels, width), bf16),
            pltpu.VMEM((classes, width), bf16),
            pltpu.VMEM((1, width), f32),
            pltpu.VMEM((cells, channels), f32),
            pltpu.SemaphoreType.DMA((5,)),
        ],
        compiler_params=PARAMS,
        name="head_grad",
    )(index("pipe"), logits, block, gated, project_t, w_head[0], class_t)
    gate_grad = lax.psum(gate_grad, "space")

    peers = lax.axis_size("x") * lax.axis_size("y")
    used = 2 * channels + depth_rows + 2 * tall
    share = up_to(-(-used // (2 * peers)), 8)
    rows = 2 * peers * share
    packed = pl.pallas_call(
        backward_kernel,
        in_specs=[SMEM] + [VMEM] * 4 + [ANY] * 3 + [VMEM] + [ANY] * 4,
        out_specs=VMEM,
        out_shape=jax.ShapeDtypeStruct((rows, broad), f32),
        scratch_shapes=[
            pltpu.VMEM((16 * columns, channels), bf16),
            pltpu.VMEM((channels, 16 * columns), bf16),
            pltpu.VMEM((channels, broad), bf16),
            pltpu.VMEM((cells, broad), f32),
            pltpu.VMEM((cells, channels), bf16),
            pltpu.VMEM((channels, broad), bf16),
            pltpu.VMEM((1, broad), f32),
            pltpu.VMEM((1, broad), f32),
            pltpu.VMEM((columns + 4, 16, BAND), f32),
            pltpu.VMEM((columns, 16, BAND), f32),
            pltpu.VMEM((columns + 4, 8, BAND), f32),
            pltpu.VMEM((16 * columns, BAND), bf16),
            pltpu.SemaphoreType.DMA((7,)),
        ],
        compiler_params=PARAMS,
        name="depthwise_grad",
    )(
        index("space"), gate_grad, squeeze, reduce_t, excite_w, cell_rows, cells_t,
        expand_w, depth_w, half, grad_block, project_t, project_grad,
    )

    halves = packed.reshape(2, peers, share, broad)
    core = lax.axis_index("core")
    swap = [(0, 1), (1, 0)]
    keep = lax.dynamic_index_in_dim(halves, core, 0, False)
    send = lax.dynamic_index_in_dim(halves, 1 - core, 0, False)
    both = (keep + lax.ppermute(send, "core", swap)).astype(bf16)
    pieces = lax.all_to_all(both, ("x", "y"), 0, 0, tiled=True)
    piece = jnp.sum(pieces.astype(f32), axis=0)
    for step in (1, 2):
        piece = piece + lax.ppermute(piece, "space", [(i, i ^ step) for i in range(space)])
    copies = jnp.broadcast_to(piece[None], pieces.shape)
    gathered = lax.all_to_all(copies, ("x", "y"), 0, 0, tiled=True)
    remote = lax.ppermute(gathered, "core", swap)
    g_expand, g_depth, g_reduce, g_excite, g_project = pl.pallas_call(
        unpack_kernel,
        in_specs=[SMEM] + [VMEM] * 2,
        out_specs=[VMEM] * 5,
        out_shape=[
            jax.ShapeDtypeStruct((1, channels, hidden), f32),
            jax.ShapeDtypeStruct((extent, extent, 1, hidden), f32),
            jax.ShapeDtypeStruct((reduced, 1, hidden), f32),
            jax.ShapeDtypeStruct((reduced, 1, hidden), f32),
            jax.ShapeDtypeStruct((1, channels, hidden), f32),
        ],
        compiler_params=PARAMS,
        name="unpack",
    )(index("core"), gathered.reshape(peers * share, broad), remote.reshape(peers * share, broad))
    return (
        g_expand,
        g_depth.transpose(2, 0, 1, 3),
        g_reduce.transpose(1, 2, 0),
        g_excite.transpose(1, 0, 2),
        g_project.transpose(0, 2, 1),
    )


def solution(mesh):
    pipe, replica, space = (mesh.shape[name] for name in ("pipe", "replica", "space"))
    side = 1
    while 2 * side * side < replica:
        side *= 2
    fine = Mesh(
        mesh.devices.reshape(pipe, replica // (2 * side), side, 2, space),
        ("pipe", "x", "y", "core", "space"),
    )
    in_specs = (P("pipe", ("x", "y", "core"), "space"),) + (P("pipe"),) * 7
    return jax.shard_map(
        shards, mesh=fine, in_specs=in_specs, out_specs=(P("pipe"),) * 5, check_vma=False
    )
```

```python
import jax
import jax.numpy as jnp
from jax import lax
from jax.experimental import pallas as pl
from jax.experimental.pallas import tpu as pltpu
from jax.sharding import Mesh
from jax.sharding import PartitionSpec as P

loss_scale = 256.0
f32 = jnp.float32
bf16 = jnp.bfloat16
LANES = 128
BAND = 384
HEAD_CHUNK = 512
STRIP = 50
WIDE = 100
TAPS = 50
VMEM = pl.BlockSpec(memory_space=pltpu.VMEM)
SMEM = pl.BlockSpec(memory_space=pltpu.SMEM)
ANY = pl.BlockSpec(memory_space=pl.ANY)
PARAMS = pltpu.CompilerParams(vmem_limit_bytes=60 * 1024 * 1024)


def up_to(size, multiple):
    return -(-size // multiple) * multiple


def started(*copies):
    made = [pltpu.make_async_copy(*copy) for copy in copies]
    for copy in made:
        copy.start()
    return made


def chunks(width, chunk, unroll, work):
    whole = width // chunk

    @pl.loop(0, whole, unroll=unroll)
    def each(part):
        work(pl.multiple_of(part * chunk, chunk), chunk)

    if width > whole * chunk:
        work(whole * chunk, width - whole * chunk)


def contract(left, right, left_dim, right_dim):
    return lax.dot_general(
        left, right, (((left_dim,), (right_dim,)), ((), ())), preferred_element_type=f32
    )


def row_window(own, rim, extent, place):
    margin = extent // 2
    window = []
    for i in range(extent):
        d = i - margin
        if d == 0:
            window.append(own)
        elif d > 0:
            window.append(pltpu.roll(jnp.where(place < d, rim, own), 8 - d, 0))
        else:
            window.append(pltpu.roll(jnp.where(place >= 8 + d, rim, own), -d, 0))
    return window


def forward_kernel(
    own_ref, before_ref, after_ref, expand_ref, depth_ref,
    cells_out, cells_t_out, mine_out, half_out, squeeze_ref,
    cells_ref, cells_t_ref, mine_ref, half_ref, left, right, expanded, sems,
):
    columns, channels = own_ref.shape[1:]
    extent, margin = 5, 2

    left[...] = jnp.zeros_like(left)
    right[...] = jnp.zeros_like(right)
    rest = channels - LANES
    for ref, base in ((own_ref, 0), (after_ref, 8), (before_ref, 14)):
        for y in range(ref.shape[0]):
            row = ref[y].astype(f32)
            left[pl.ds(base + y, columns, stride=16), :] = row[:, :LANES]
            right[pl.ds(base + y, columns, stride=16), :] = jnp.concatenate(
                [row[:, LANES:], jnp.zeros((columns, LANES - rest), f32)], axis=1
            )
    low, high = left[...], right[...]
    cells_ref[:, :LANES] = low.astype(bf16)
    cells_ref[:, LANES:] = high[:, :rest].astype(bf16)
    for start in range(0, 16 * columns, 320):
        cells_t_ref[:LANES, start : start + 320] = left[start : start + 320, :].T.astype(bf16)
        cells_t_ref[LANES:, start : start + 320] = right[start : start + 320, :].T[:rest].astype(
            bf16
        )
    mine_ref[:, :LANES] = (
        low.reshape(columns, 16, LANES)[:, :8].reshape(8 * columns, LANES).astype(bf16)
    )
    mine_ref[:, LANES:] = (
        high.reshape(columns, 16, LANES)[:, :8]
        .reshape(8 * columns, LANES)[:, :rest]
        .astype(bf16)
    )
    sends = started(
        (cells_ref, cells_out, sems.at[0]),
        (cells_t_ref, cells_t_out, sems.at[1]),
        (mine_ref, mine_out, sems.at[2]),
    )
    edge = jnp.zeros((margin, 16, expanded.shape[2]), f32)
    expanded[:margin] = edge
    expanded[margin + columns :] = edge

    @pl.loop(0, columns // WIDE)
    def expand(part):
        rows = pl.ds(pl.multiple_of(part * 16 * WIDE, 16 * WIDE), 16 * WIDE)
        half = jnp.dot(cells_ref[rows, :], expand_ref[...], preferred_element_type=f32)
        value = half + half * jnp.tanh(half)
        expanded[pl.ds(margin + part * WIDE, WIDE)] = value.reshape(WIDE, 16, half.shape[1])

    place = lax.broadcasted_iota(jnp.int32, (8, LANES), 0)

    @pl.loop(0, expanded.shape[2] // LANES)
    def convolve(tile):
        lanes = pl.ds(pl.multiple_of(tile * LANES, LANES), LANES)
        weight = [
            [depth_ref[i * extent + j : i * extent + j + 1, lanes] for j in range(extent)]
            for i in range(extent)
        ]

        def strip(number, total):
            x0 = number * STRIP
            sums = {}
            for k in range(STRIP + extent - 1):
                window = row_window(
                    expanded[x0 + k, :8, lanes], expanded[x0 + k, 8:, lanes], extent, place
                )
                for j in range(extent):
                    x = k - j
                    if 0 <= x < STRIP:
                        term = window[0] * weight[0][j]
                        for i in range(1, extent):
                            term = term + window[i] * weight[i][j]
                        sums[x] = term if x not in sums else sums[x] + term
                x = k - extent + 1
                if x >= 0:
                    half = 0.5 * sums.pop(x)
                    half_ref[pl.ds(pl.multiple_of((x0 + x) * 8, 8), 8), lanes] = half
                    total = total + (half + half * jnp.tanh(half))
            return total

        total = lax.fori_loop(0, columns // STRIP, strip, jnp.zeros((8, LANES), f32))
        squeeze_ref[:, lanes] = jnp.sum(total, axis=0, keepdims=True)
        pltpu.make_async_copy(
            half_ref.at[:, lanes], half_out.at[:, lanes], sems.at[3 + tile]
        ).start()

    for tile in range(half_ref.shape[1] // LANES):
        lanes = slice(tile * LANES, (tile + 1) * LANES)
        pltpu.make_async_copy(
            half_ref.at[:, lanes], half_out.at[:, lanes], sems.at[3 + tile]
        ).wait()
    for send in sends:
        send.wait()


def gate_of(squeeze, reduce_t, excite):
    reduced_in = jnp.sum(reduce_t * squeeze, axis=1, keepdims=True)
    reduced = reduced_in * jax.nn.sigmoid(reduced_in)
    gate = jax.nn.sigmoid(jnp.sum(excite * reduced, axis=0, keepdims=True))
    return reduced_in, reduced, gate


def head_kernel(
    half_in, squeeze_ref, reduce_ref, excite_ref, project_in, mine_in, head_in, class_in,
    logits_ref, gated_out, block_ref,
    half_ref, gated_ref, project_ref, mine_ref, head_ref, class_ref, gate_row, sums,
    sems, part_sems,
):
    cells = half_ref.shape[0]
    classes = class_ref.shape[0]

    def piece(part):
        rows = pl.ds(pl.multiple_of(part * 80, 80), 80)
        return half_in.at[rows, :], half_ref.at[rows, :], part_sems.at[part]

    for part in range(cells // 80):
        started(piece(part))
    project_copy, mine_copy, head_copy, class_copy = started(
        (project_in, project_ref, sems.at[3]),
        (mine_in, mine_ref, sems.at[4]),
        (head_in, head_ref, sems.at[0]),
        (class_in, class_ref, sems.at[1]),
    )
    cell_total = 4 * cells
    gate_row[...] = gate_of(squeeze_ref[...] / cell_total, reduce_ref[...], excite_ref[...])[2]

    @pl.loop(0, cells // 80)
    def gating(part):
        pltpu.make_async_copy(*piece(part)).wait()
        rows = pl.ds(pl.multiple_of(part * 80, 80), 80)
        half = half_ref[rows, :]
        gated_ref[rows, :] = ((half + half * jnp.tanh(half)) * gate_row[...]).astype(bf16)

    (send,) = started((gated_ref, gated_out, sems.at[2]))
    project_copy.wait()
    mine_copy.wait()
    residual = contract(gated_ref[...], project_ref[...], 1, 1)
    block = (mine_ref[...].astype(f32) + residual).astype(bf16)
    block_ref[...] = (0.5 * block.astype(f32)).astype(bf16)

    def head(first, count):
        lanes = pl.ds(first, count)
        half = jnp.dot(block_ref[...], head_ref[:, lanes], preferred_element_type=f32)
        act = half + half * jnp.tanh(half)
        sums[:, lanes] = jnp.sum(act.reshape(cells // 8, 8, count), axis=0)

    head_copy.wait()
    chunks(head_ref.shape[1], HEAD_CHUNK, 5, head)
    class_copy.wait()
    pooled = sums[...]
    high = pooled.astype(bf16).astype(f32)
    both = jnp.concatenate([high, pooled - high], axis=0).astype(bf16)
    partial = jnp.sum(contract(both, class_ref[...], 1, 1), axis=0, keepdims=True)
    logits_ref[...] = jnp.zeros_like(logits_ref)
    for rank in range(logits_ref.shape[0]):
        logits_ref[rank, :, :classes] = partial / cell_total
    send.wait()


def head_grad_kernel(
    which_ref, logits_ref, block_in, gated_in, project_in, head_in, class_in,
    grad_ref, project_grad_ref, gate_grad_ref,
    block_ref, gated_ref, project_ref, head_ref, class_ref, pooled, total, sems,
):
    class_copy, block_copy, head_copy, gated_copy, project_copy = started(
        (class_in, class_ref, sems.at[0]),
        (block_in, block_ref, sems.at[1]),
        (head_in, head_ref, sems.at[2]),
        (gated_in, gated_ref, sems.at[3]),
        (project_in, project_ref, sems.at[4]),
    )
    cells = block_ref.shape[0]
    classes = class_ref.shape[0]
    total[...] = jnp.zeros_like(total)

    ranks, wide = logits_ref.shape[0], logits_ref.shape[2]
    valid = lax.broadcasted_iota(jnp.int32, (1, wide), 1) < classes
    teacher, student = logits_ref[0], logits_ref[1]
    for rank in range(2, ranks, 2):
        teacher = teacher + logits_ref[rank]
        student = student + logits_ref[rank + 1]
    exp_teacher = jnp.where(valid, jnp.exp(teacher), 0.0)
    prob = exp_teacher / jnp.sum(exp_teacher, axis=1, keepdims=True)
    log_sum = jnp.log(
        jnp.sum(jnp.where(valid, jnp.exp(student), 0.0), axis=1, keepdims=True)
    )
    logprob = student - log_sum
    cross = jnp.sum(prob * logprob, axis=1, keepdims=True)
    teacher_grad = loss_scale * prob * (cross - logprob)
    student_grad = loss_scale * (jnp.exp(logprob) - prob)
    grad = jnp.where(which_ref[0] == 0, teacher_grad, student_grad)
    grad = jnp.where(valid, grad, 0.0)
    grad = jnp.broadcast_to(grad, (16, wide)).astype(bf16)[:, :classes]
    class_copy.wait()
    pooled[...] = contract(grad, class_ref[...], 1, 0)[:1] * (0.5 / (4 * cells))

    def head(first, count):
        lanes = pl.ds(first, count)
        weight = head_ref[:, lanes]
        half = jnp.dot(block_ref[...], weight, preferred_element_type=f32)
        t = jnp.tanh(half)
        slope = (1.0 + t) * (1.0 + (half - half * t))
        grad_head = (slope * pooled[:, lanes]).astype(bf16)
        total[...] += contract(grad_head, weight, 1, 1)

    block_copy.wait()
    head_copy.wait()
    chunks(head_ref.shape[1], HEAD_CHUNK, 10, head)
    grad_block = total[...]
    grad_ref[...] = grad_block.astype(bf16)
    gated_copy.wait()
    project_copy.wait()
    project_grad = jnp.dot(grad_block.T.astype(bf16), gated_ref[...], preferred_element_type=f32)
    project_grad_ref[...] = project_grad
    gate_grad_ref[...] = jnp.sum(
        project_ref[...].astype(f32) * project_grad, axis=0, keepdims=True
    )


def backward_kernel(
    place_ref, gate_grad_ref, squeeze_ref, reduce_ref, excite_ref, cells_in, cells_t_in,
    expand_in, depth_ref, half_in, grad_in, project_in, project_grad_in,
    keep_ref, send_ref,
    out_ref,
    cells_ref, cells_t_ref, expand_ref, half_ref, grad_ref, project_ref, gate_row, pool_row,
    expanded, slope, grad_depth, grad_expand, sems,
):
    channels = grad_in.shape[1]
    peers, share, hidden = keep_ref.shape
    half_rows = peers * share
    depth_base = channels
    excite_base = channels + depth_ref.shape[0]
    project_base = half_rows
    reduce_base = half_rows + channels
    arriving = started(
        (cells_in, cells_ref, sems.at[0]),
        (expand_in, expand_ref, sems.at[1]),
        (grad_in, grad_ref, sems.at[2]),
        (project_in, project_ref, sems.at[3]),
        (half_in, half_ref, sems.at[4]),
        (cells_t_in, cells_t_ref, sems.at[5]),
        (project_grad_in, out_ref.at[project_base:reduce_base, :], sems.at[6]),
    )
    cells = half_ref.shape[0]
    columns = cells // 8
    reduced_rows = reduce_ref.shape[0]
    extent, margin = 5, 2
    cell_total = 4 * cells
    excite_end = excite_base + reduced_rows
    reduce_end = reduce_base + reduced_rows

    squeeze = squeeze_ref[...] / cell_total
    reduced_in, reduced, gate = gate_of(squeeze, reduce_ref[...], excite_ref[...])
    grad_excite = (1.0 - gate) * gate_grad_ref[...]
    sigma = jax.nn.sigmoid(reduced_in)
    grad_reduced = jnp.sum(excite_ref[...] * grad_excite, axis=1, keepdims=True) * (
        sigma * (1.0 + reduced_in * (1.0 - sigma))
    )
    back_pool = jnp.sum(reduce_ref[...] * grad_reduced, axis=0, keepdims=True)
    gate_row[...] = 0.25 * gate
    pool_row[...] = back_pool * (0.25 / cell_total)
    once = jnp.where(place_ref[0] == 0, 1.0, 0.0)
    out_ref[excite_base:excite_end, :] = reduced * (grad_excite * once)
    out_ref[reduce_base:reduce_end, :] = grad_reduced * (squeeze * once)
    for first, last in ((excite_end, half_rows), (reduce_end, 2 * half_rows)):
        if first < last:
            out_ref[first:last, :] = jnp.zeros((last - first, out_ref.shape[1]), f32)
    edge = jnp.zeros((margin, 16, BAND), f32)
    expanded[:margin] = edge
    expanded[margin + columns :] = edge
    grad_depth[:margin] = edge[:, :8]
    grad_depth[margin + columns :] = edge[:, :8]

    for copy in arriving[:2]:
        copy.wait()

    @pl.loop(0, out_ref.shape[1] // BAND)
    def each(step):
        backward_band(
            step, arriving[2:], depth_base, excite_base,
            cells_ref, cells_t_ref, expand_ref, depth_ref, half_ref, grad_ref, project_ref,
            out_ref, gate_row, pool_row, expanded, slope, grad_depth, grad_expand,
        )

    core = place_ref[1]
    mine = pl.ds(pl.multiple_of(core * half_rows, half_rows), half_rows)
    theirs = pl.ds(pl.multiple_of((1 - core) * half_rows, half_rows), half_rows)
    keep_ref[...] = out_ref[mine, :][:, :hidden].reshape(keep_ref.shape)
    send_ref[...] = out_ref[theirs, :][:, :hidden].astype(bf16).reshape(send_ref.shape)


def backward_band(
    step, arriving, depth_base, excite_base,
    cells_ref, cells_t_ref, expand_ref, depth_ref, half_ref, grad_ref, project_ref,
    out_ref, gate_row, pool_row, expanded, slope, grad_depth, grad_expand,
):
    columns = half_ref.shape[0] // 8
    channels = grad_ref.shape[1]
    extent, margin = 5, 2
    start = pl.multiple_of(step * BAND, BAND)
    band = pl.ds(start, BAND)
    gate = gate_row[:, band]
    back_pool = pool_row[:, band]

    @pl.loop(0, columns // WIDE)
    def elements(part):
        rows = pl.ds(pl.multiple_of(part * 16 * WIDE, 16 * WIDE), 16 * WIDE)
        half = jnp.dot(cells_ref[rows, :], expand_ref[:, band], preferred_element_type=f32)
        t = jnp.tanh(half)
        turn = half * t
        expanded[pl.ds(margin + part * WIDE, WIDE)] = (half + turn).reshape(WIDE, 16, BAND)
        value = (1.0 + t) * (1.0 + (half - turn))
        slope[pl.ds(part * WIDE, WIDE)] = value.reshape(WIDE, 16, BAND)

    @pl.when(step == 0)
    def arrive():
        for copy in arriving:
            copy.wait()

    @pl.loop(0, columns // WIDE)
    def gradients(part):
        rows = pl.ds(pl.multiple_of(part * 8 * WIDE, 8 * WIDE), 8 * WIDE)
        grad_gated = jnp.dot(
            grad_ref[rows, :], project_ref[:, band], preferred_element_type=f32
        )
        half = half_ref[rows, band]
        t = jnp.tanh(half)
        value = (grad_gated * gate + back_pool) * ((1.0 + t) * (1.0 + (half - half * t)))
        grad_depth[pl.ds(margin + part * WIDE, WIDE)] = value.reshape(WIDE, 8, BAND)

    place = lax.broadcasted_iota(jnp.int32, (8, LANES), 0)

    @pl.loop(0, BAND // LANES)
    def convolve(tile):
        lanes = pl.ds(pl.multiple_of(tile * LANES, LANES), LANES)
        out_lanes = pl.ds(pl.multiple_of(start + tile * LANES, LANES), LANES)

        def taps(number, sums):
            sums = [list(line) for line in sums]
            base = margin + number * TAPS
            grads = {}
            for k in range(TAPS):
                window = row_window(
                    expanded[base + k, :8, lanes], expanded[base + k, 8:, lanes], extent, place
                )
                for j in range(extent):
                    place_x = k - j
                    if place_x not in grads:
                        grads[place_x] = grad_depth[base + place_x + margin, :, lanes]
                    for i in range(extent):
                        sums[i][j] = sums[i][j] + window[i] * grads[place_x]
            return tuple(tuple(line) for line in sums)

        zero = jnp.zeros((8, LANES), f32)
        sums = lax.fori_loop(0, columns // TAPS, taps, ((zero,) * extent,) * extent)
        for i in range(extent):
            for j in range(extent):
                row = depth_base + i * extent + j
                out_ref[row : row + 1, out_lanes] = 2.0 * jnp.sum(sums[i][j], axis=0, keepdims=True)
        for row in range(depth_base + extent * extent, excite_base):
            out_ref[row : row + 1, out_lanes] = jnp.zeros((1, LANES), f32)

        weight = [
            [depth_ref[i * extent + j : i * extent + j + 1, out_lanes] for j in range(extent)]
            for i in range(extent)
        ]

        @pl.loop(0, columns // STRIP)
        def spread(number):
            x0 = number * STRIP
            grads = [grad_depth[x0 + k, :, lanes] for k in range(extent - 1)]
            for x in range(STRIP):
                grads.append(grad_depth[x0 + x + extent - 1, :, lanes])
                whole, far = None, None
                for i in range(extent):
                    term = grads[x + extent - 1] * weight[i][0]
                    for j in range(1, extent):
                        term = term + grads[x + extent - 1 - j] * weight[i][j]
                    d = i - margin
                    if d != 0:
                        term = pltpu.roll(term, d % 8, 0)
                        inside = place >= d if d > 0 else place < 8 + d
                        leave = jnp.where(inside, 0.0, term)
                        far = leave if far is None else far + leave
                    whole = term if whole is None else whole + term
                near = whole - far
                near = near * slope[x0 + x, :8, lanes]
                far = far * slope[x0 + x, 8:, lanes]
                rows = pl.ds(pl.multiple_of((x0 + x) * 16, 16), 16)
                grad_expand[rows, lanes] = jnp.concatenate([near, far], axis=0).astype(bf16)

    out_ref[:channels, band] = jnp.dot(
        cells_t_ref[...], grad_expand[...], preferred_element_type=f32
    )


def unpack_kernel(
    core_ref, own_ref, other_ref,
    expand_ref, depth_ref, reduce_ref, excite_ref, project_ref,
):
    channels = expand_ref.shape[1]
    extent = depth_ref.shape[0]
    reduced = excite_ref.shape[0]
    excite_base = up_to(extent * extent, 8)

    def arrange(first, second):
        expand_ref[0] = first[:channels, :]
        project_ref[0] = second[:channels, :]
        for i in range(extent):
            for j in range(extent):
                row = channels + i * extent + j
                depth_ref[i, j] = first[row : row + 1, :]
        for r in range(reduced):
            row = channels + excite_base + r
            excite_ref[r] = first[row : row + 1, :]
            row = channels + r
            reduce_ref[r] = second[row : row + 1, :]

    @pl.when(core_ref[0] == 0)
    def even():
        arrange(own_ref, other_ref)

    @pl.when(core_ref[0] != 0)
    def odd():
        arrange(other_ref, own_ref)


def shards(views, w_expand, w_depth, w_reduce, w_excite, w_project, w_head, w_class):
    own = views[0, 0]
    height, columns, channels = own.shape
    hidden = w_expand.shape[2]
    reduced = w_reduce.shape[2]
    extent = w_depth.shape[1]
    width = w_head.shape[2]
    classes = w_class.shape[2]
    cells = height * columns
    space = lax.axis_size("space")
    broad = up_to(hidden, BAND)
    tall = up_to(reduced, 8)

    up = [(i, i + 1) for i in range(space - 1)]
    down = [(i + 1, i) for i in range(space - 1)]
    before = lax.ppermute(own[height - 2 :], "space", up)
    after = lax.ppermute(own[:2], "space", down)

    fill = broad - hidden
    expand_w = jnp.pad(w_expand[0] * bf16(0.5), ((0, 0), (0, fill)))
    depth_w = jnp.pad(
        w_depth[0].reshape(extent * extent, hidden).astype(f32),
        ((0, up_to(extent * extent, 8) - extent * extent), (0, fill)),
    )
    reduce_t = jnp.pad(w_reduce[0].T.astype(f32), ((0, tall - reduced), (0, fill)))
    excite_w = jnp.pad(w_excite[0].astype(f32), ((0, tall - reduced), (0, fill)))
    class_t = w_class[0].T
    project_t = jnp.pad(w_project[0].T, ((0, 0), (0, fill)))

    depth_rows = depth_w.shape[0]
    cell_rows, cells_t, mine, half, squeeze = pl.pallas_call(
        forward_kernel,
        in_specs=[VMEM] * 5,
        out_specs=[ANY] * 4 + [VMEM],
        out_shape=[
            jax.ShapeDtypeStruct((16 * columns, channels), bf16),
            jax.ShapeDtypeStruct((channels, 16 * columns), bf16),
            jax.ShapeDtypeStruct((cells, channels), bf16),
            jax.ShapeDtypeStruct((cells, broad), f32),
            jax.ShapeDtypeStruct((1, broad), f32),
        ],
        scratch_shapes=[
            pltpu.VMEM((16 * columns, channels), bf16),
            pltpu.VMEM((channels, 16 * columns), bf16),
            pltpu.VMEM((cells, channels), bf16),
            pltpu.VMEM((cells, broad), f32),
            pltpu.VMEM((16 * columns, LANES), f32),
            pltpu.VMEM((16 * columns, LANES), f32),
            pltpu.VMEM((columns + 4, 16, broad), f32),
            pltpu.SemaphoreType.DMA((3 + broad // LANES,)),
        ],
        compiler_params=PARAMS,
        name="expand_depthwise",
    )(own, before, after, expand_w, depth_w)
    squeeze = lax.psum(squeeze, "space")

    ranks = 2 * space
    logits, gated, block = pl.pallas_call(
        head_kernel,
        in_specs=[ANY] + [VMEM] * 3 + [ANY] * 4,
        out_specs=[VMEM, ANY, VMEM],
        out_shape=[
            jax.ShapeDtypeStruct((ranks, 1, up_to(classes, LANES)), f32),
            jax.ShapeDtypeStruct((cells, broad), bf16),
            jax.ShapeDtypeStruct((cells, channels), bf16),
        ],
        scratch_shapes=[
            pltpu.VMEM((cells, broad), f32),
            pltpu.VMEM((cells, broad), bf16),
            pltpu.VMEM((channels, broad), bf16),
            pltpu.VMEM((cells, channels), bf16),
            pltpu.VMEM((channels, width), bf16),
            pltpu.VMEM((classes, width), bf16),
            pltpu.VMEM((1, broad), f32),
            pltpu.VMEM((8, width), f32),
            pltpu.SemaphoreType.DMA((5,)),
            pltpu.SemaphoreType.DMA((cells // 80,)),
        ],
        compiler_params=PARAMS,
        name="project_head",
    )(half, squeeze, reduce_t, excite_w, project_t, mine, w_head[0], class_t)
    logits = lax.all_to_all(logits, ("space", "pipe"), 0, 0, tiled=True)

    def index(name):
        return lax.axis_index(name).astype(jnp.int32).reshape(1)

    grad_block, project_grad, gate_grad = pl.pallas_call(
        head_grad_kernel,
        in_specs=[SMEM, VMEM] + [ANY] * 5,
        out_specs=[VMEM] * 3,
        out_shape=[
            jax.ShapeDtypeStruct((cells, channels), bf16),
            jax.ShapeDtypeStruct((channels, broad), f32),
            jax.ShapeDtypeStruct((1, broad), f32),
        ],
        scratch_shapes=[
            pltpu.VMEM((cells, channels), bf16),
            pltpu.VMEM((cells, broad), bf16),
            pltpu.VMEM((channels, broad), bf16),
            pltpu.VMEM((channels, width), bf16),
            pltpu.VMEM((classes, width), bf16),
            pltpu.VMEM((1, width), f32),
            pltpu.VMEM((cells, channels), f32),
            pltpu.SemaphoreType.DMA((5,)),
        ],
        compiler_params=PARAMS,
        name="head_grad",
    )(index("pipe"), logits, block, gated, project_t, w_head[0], class_t)
    gate_grad = lax.psum(gate_grad, "space")

    peers = lax.axis_size("x") * lax.axis_size("y")
    share = up_to(-(-(channels + depth_rows + tall) // peers), 16)
    half_rows = peers * share
    keep, send = pl.pallas_call(
        backward_kernel,
        in_specs=[SMEM] + [VMEM] * 4 + [ANY] * 3 + [VMEM] + [ANY] * 4,
        out_specs=[VMEM, VMEM],
        out_shape=[
            jax.ShapeDtypeStruct((peers, share, hidden), f32),
            jax.ShapeDtypeStruct((peers, share, hidden), bf16),
        ],
        scratch_shapes=[
            pltpu.VMEM((2 * half_rows, broad), f32),
            pltpu.VMEM((16 * columns, channels), bf16),
            pltpu.VMEM((channels, 16 * columns), bf16),
            pltpu.VMEM((channels, broad), bf16),
            pltpu.VMEM((cells, broad), f32),
            pltpu.VMEM((cells, channels), bf16),
            pltpu.VMEM((channels, broad), bf16),
            pltpu.VMEM((1, broad), f32),
            pltpu.VMEM((1, broad), f32),
            pltpu.VMEM((columns + 4, 16, BAND), f32),
            pltpu.VMEM((columns, 16, BAND), f32),
            pltpu.VMEM((columns + 4, 8, BAND), f32),
            pltpu.VMEM((16 * columns, BAND), bf16),
            pltpu.SemaphoreType.DMA((7,)),
        ],
        compiler_params=PARAMS,
        name="depthwise_grad",
    )(
        jnp.concatenate([index("space"), index("core")]), gate_grad, squeeze, reduce_t, excite_w, cell_rows, cells_t,
        expand_w, depth_w, half, grad_block, project_t, project_grad,
    )

    swap = [(0, 1), (1, 0)]
    both = (keep + lax.ppermute(send, "core", swap).astype(f32)).astype(bf16)
    pieces = lax.all_to_all(both, ("x", "y"), 0, 0, tiled=True)
    piece = jnp.sum(pieces.astype(f32), axis=0)
    for step in (1, 3):
        piece = piece + lax.ppermute(piece, "space", [(i, i ^ step) for i in range(space)])
    copies = jnp.broadcast_to(piece[None], pieces.shape)
    gathered = lax.all_to_all(copies, ("x", "y"), 0, 0, tiled=True)
    remote = lax.ppermute(gathered, "core", swap)
    g_expand, g_depth, g_reduce, g_excite, g_project = pl.pallas_call(
        unpack_kernel,
        in_specs=[SMEM, VMEM, VMEM],
        out_specs=[VMEM] * 5,
        out_shape=[
            jax.ShapeDtypeStruct((1, channels, hidden), f32),
            jax.ShapeDtypeStruct((extent, extent, 1, hidden), f32),
            jax.ShapeDtypeStruct((reduced, 1, hidden), f32),
            jax.ShapeDtypeStruct((reduced, 1, hidden), f32),
            jax.ShapeDtypeStruct((1, channels, hidden), f32),
        ],
        compiler_params=pltpu.CompilerParams(vmem_limit_bytes=24 * 1024 * 1024),
        name="unpack",
    )(index("core"), gathered.reshape(half_rows, hidden), remote.reshape(half_rows, hidden))
    return (
        g_expand,
        g_depth.transpose(2, 0, 1, 3),
        g_reduce.transpose(1, 2, 0),
        g_excite.transpose(1, 0, 2),
        g_project.transpose(0, 2, 1),
    )


def solution(mesh):
    pipe, replica, space = (mesh.shape[name] for name in ("pipe", "replica", "space"))
    side = 1
    while 2 * side * side < replica:
        side *= 2
    fine = Mesh(
        mesh.devices.reshape(pipe, replica // (2 * side), side, 2, space),
        ("pipe", "x", "y", "core", "space"),
    )
    in_specs = (P("pipe", ("x", "y", "core"), "space"),) + (P("pipe"),) * 7
    return jax.shard_map(
        shards, mesh=fine, in_specs=in_specs, out_specs=(P("pipe"),) * 5, check_vma=False
    )
```

```python
import jax
import jax.numpy as jnp
from jax import lax
from jax.experimental import pallas as pl
from jax.experimental.pallas import tpu as pltpu
from jax.sharding import Mesh
from jax.sharding import PartitionSpec as P

loss_scale = 256.0
f32 = jnp.float32
bf16 = jnp.bfloat16
LANES = 128
BAND = 1152
HEAD_CHUNK = 512
STRIP = 100
WIDE = 100
TAPS = 50
VMEM = pl.BlockSpec(memory_space=pltpu.VMEM)
SMEM = pl.BlockSpec(memory_space=pltpu.SMEM)
ANY = pl.BlockSpec(memory_space=pl.ANY)
PARAMS = pltpu.CompilerParams(vmem_limit_bytes=60 * 1024 * 1024)


def up_to(size, multiple):
    return -(-size // multiple) * multiple


def started(*copies):
    made = [pltpu.make_async_copy(*copy) for copy in copies]
    for copy in made:
        copy.start()
    return made


def chunks(width, chunk, unroll, work):
    whole = width // chunk

    @pl.loop(0, whole, unroll=unroll)
    def each(part):
        work(pl.multiple_of(part * chunk, chunk), chunk)

    if width > whole * chunk:
        work(whole * chunk, width - whole * chunk)


def contract(left, right, left_dim, right_dim):
    return lax.dot_general(
        left, right, (((left_dim,), (right_dim,)), ((), ())), preferred_element_type=f32
    )


def row_window(own, rim, extent, place):
    margin = extent // 2
    window = []
    for i in range(extent):
        d = i - margin
        if d == 0:
            window.append(own)
        elif d > 0:
            window.append(pltpu.roll(jnp.where(place < d, rim, own), 8 - d, 0))
        else:
            window.append(pltpu.roll(jnp.where(place >= 8 + d, rim, own), -d, 0))
    return window


def forward_kernel(
    own_ref, before_ref, after_ref, expand_ref, depth_ref,
    cells_out, cells_t_out, mine_out, half_out, squeeze_ref,
    cells_ref, cells_t_ref, mine_ref, half_ref, left, right, expanded, sems,
):
    columns, channels = own_ref.shape[1:]
    extent, margin = 5, 2

    left[...] = jnp.zeros_like(left)
    right[...] = jnp.zeros_like(right)
    rest = channels - LANES
    for ref, base in ((own_ref, 0), (after_ref, 8), (before_ref, 14)):
        for y in range(ref.shape[0]):
            row = ref[y].astype(f32)
            left[pl.ds(base + y, columns, stride=16), :] = row[:, :LANES]
            right[pl.ds(base + y, columns, stride=16), :] = jnp.concatenate(
                [row[:, LANES:], jnp.zeros((columns, LANES - rest), f32)], axis=1
            )
    low, high = left[...], right[...]
    cells_ref[:, :LANES] = low.astype(bf16)
    cells_ref[:, LANES:] = high[:, :rest].astype(bf16)
    for start in range(0, 16 * columns, 320):
        cells_t_ref[:LANES, start : start + 320] = left[start : start + 320, :].T.astype(bf16)
        cells_t_ref[LANES:, start : start + 320] = right[start : start + 320, :].T[:rest].astype(
            bf16
        )
    mine_ref[:, :LANES] = (
        low.reshape(columns, 16, LANES)[:, :8].reshape(8 * columns, LANES).astype(bf16)
    )
    mine_ref[:, LANES:] = (
        high.reshape(columns, 16, LANES)[:, :8]
        .reshape(8 * columns, LANES)[:, :rest]
        .astype(bf16)
    )
    sends = started(
        (cells_ref, cells_out, sems.at[0]),
        (cells_t_ref, cells_t_out, sems.at[1]),
        (mine_ref, mine_out, sems.at[2]),
    )
    edge = jnp.zeros((margin, 16, expanded.shape[2]), f32)
    expanded[:margin] = edge
    expanded[margin + columns :] = edge

    @pl.loop(0, columns // WIDE)
    def expand(part):
        rows = pl.ds(pl.multiple_of(part * 16 * WIDE, 16 * WIDE), 16 * WIDE)
        half = jnp.dot(cells_ref[rows, :], expand_ref[...], preferred_element_type=f32)
        value = half + half * jnp.tanh(half)
        expanded[pl.ds(margin + part * WIDE, WIDE)] = value.reshape(WIDE, 16, half.shape[1])

    place = lax.broadcasted_iota(jnp.int32, (8, LANES), 0)

    @pl.loop(0, expanded.shape[2] // LANES)
    def convolve(tile):
        lanes = pl.ds(pl.multiple_of(tile * LANES, LANES), LANES)
        weight = [
            [depth_ref[i * extent + j : i * extent + j + 1, lanes] for j in range(extent)]
            for i in range(extent)
        ]

        def strip(number, total):
            x0 = number * STRIP
            sums = {}
            for k in range(STRIP + extent - 1):
                window = row_window(
                    expanded[x0 + k, :8, lanes], expanded[x0 + k, 8:, lanes], extent, place
                )
                for j in range(extent):
                    x = k - j
                    if 0 <= x < STRIP:
                        term = window[0] * weight[0][j]
                        for i in range(1, extent):
                            term = term + window[i] * weight[i][j]
                        sums[x] = term if x not in sums else sums[x] + term
                x = k - extent + 1
                if x >= 0:
                    half = 0.5 * sums.pop(x)
                    half_ref[pl.ds(pl.multiple_of((x0 + x) * 8, 8), 8), lanes] = half
                    total = total + (half + half * jnp.tanh(half))
            return total

        total = lax.fori_loop(0, columns // STRIP, strip, jnp.zeros((8, LANES), f32))
        squeeze_ref[:, lanes] = jnp.sum(total, axis=0, keepdims=True)
        pltpu.make_async_copy(
            half_ref.at[:, lanes], half_out.at[:, lanes], sems.at[3 + tile]
        ).start()

    for tile in range(half_ref.shape[1] // LANES):
        lanes = slice(tile * LANES, (tile + 1) * LANES)
        pltpu.make_async_copy(
            half_ref.at[:, lanes], half_out.at[:, lanes], sems.at[3 + tile]
        ).wait()
    for send in sends:
        send.wait()


def gate_of(squeeze, reduce_t, excite):
    reduced_in = jnp.sum(reduce_t * squeeze, axis=1, keepdims=True)
    reduced = reduced_in * jax.nn.sigmoid(reduced_in)
    gate = jax.nn.sigmoid(jnp.sum(excite * reduced, axis=0, keepdims=True))
    return reduced_in, reduced, gate


def head_kernel(
    half_in, squeeze_ref, reduce_ref, excite_ref, project_in, mine_in, head_in, class_in,
    logits_ref, gated_out, block_ref,
    half_ref, gated_ref, project_ref, mine_ref, head_ref, class_ref, gate_row, sums,
    sems, part_sems,
):
    cells = half_ref.shape[0]
    classes = class_ref.shape[0]

    def piece(part):
        rows = pl.ds(pl.multiple_of(part * 80, 80), 80)
        return half_in.at[rows, :], half_ref.at[rows, :], part_sems.at[part]

    for part in range(cells // 80):
        started(piece(part))
    project_copy, mine_copy, head_copy, class_copy = started(
        (project_in, project_ref, sems.at[3]),
        (mine_in, mine_ref, sems.at[4]),
        (head_in, head_ref, sems.at[0]),
        (class_in, class_ref, sems.at[1]),
    )
    cell_total = 4 * cells
    gate_row[...] = gate_of(squeeze_ref[...] / cell_total, reduce_ref[...], excite_ref[...])[2]

    @pl.loop(0, cells // 80)
    def gating(part):
        pltpu.make_async_copy(*piece(part)).wait()
        rows = pl.ds(pl.multiple_of(part * 80, 80), 80)
        half = half_ref[rows, :]
        gated_ref[rows, :] = ((half + half * jnp.tanh(half)) * gate_row[...]).astype(bf16)

    (send,) = started((gated_ref, gated_out, sems.at[2]))
    project_copy.wait()
    mine_copy.wait()
    residual = contract(gated_ref[...], project_ref[...], 1, 1)
    block = (mine_ref[...].astype(f32) + residual).astype(bf16)
    block_ref[...] = (0.5 * block.astype(f32)).astype(bf16)

    def head(first, count):
        lanes = pl.ds(first, count)
        half = jnp.dot(block_ref[...], head_ref[:, lanes], preferred_element_type=f32)
        act = half + half * jnp.tanh(half)
        sums[:, lanes] = jnp.sum(act.reshape(cells // 8, 8, count), axis=0)

    head_copy.wait()
    chunks(head_ref.shape[1], HEAD_CHUNK, 5, head)
    class_copy.wait()
    pooled = sums[...]
    high = pooled.astype(bf16).astype(f32)
    both = jnp.concatenate([high, pooled - high], axis=0).astype(bf16)
    partial = jnp.sum(contract(both, class_ref[...], 1, 1), axis=0, keepdims=True)
    logits_ref[...] = jnp.zeros_like(logits_ref)
    for rank in range(logits_ref.shape[0]):
        logits_ref[rank, :, :classes] = partial / cell_total
    send.wait()


def head_grad_kernel(
    which_ref, logits_ref, block_in, gated_in, project_in, head_in, class_in,
    grad_ref, project_grad_ref, gate_grad_ref,
    block_ref, gated_ref, project_ref, head_ref, class_ref, pooled, total, sems,
):
    class_copy, block_copy, head_copy, gated_copy, project_copy = started(
        (class_in, class_ref, sems.at[0]),
        (block_in, block_ref, sems.at[1]),
        (head_in, head_ref, sems.at[2]),
        (gated_in, gated_ref, sems.at[3]),
        (project_in, project_ref, sems.at[4]),
    )
    cells = block_ref.shape[0]
    classes = class_ref.shape[0]
    total[...] = jnp.zeros_like(total)

    ranks, wide = logits_ref.shape[0], logits_ref.shape[2]
    valid = lax.broadcasted_iota(jnp.int32, (1, wide), 1) < classes
    teacher, student = logits_ref[0], logits_ref[1]
    for rank in range(2, ranks, 2):
        teacher = teacher + logits_ref[rank]
        student = student + logits_ref[rank + 1]
    exp_teacher = jnp.where(valid, jnp.exp(teacher), 0.0)
    prob = exp_teacher / jnp.sum(exp_teacher, axis=1, keepdims=True)
    log_sum = jnp.log(
        jnp.sum(jnp.where(valid, jnp.exp(student), 0.0), axis=1, keepdims=True)
    )
    logprob = student - log_sum
    cross = jnp.sum(prob * logprob, axis=1, keepdims=True)
    teacher_grad = loss_scale * prob * (cross - logprob)
    student_grad = loss_scale * (jnp.exp(logprob) - prob)
    grad = jnp.where(which_ref[0] == 0, teacher_grad, student_grad)
    grad = jnp.where(valid, grad, 0.0)
    grad = jnp.broadcast_to(grad, (16, wide)).astype(bf16)[:, :classes]
    class_copy.wait()
    pooled[...] = contract(grad, class_ref[...], 1, 0)[:1] * (0.5 / (4 * cells))

    def head(first, count):
        lanes = pl.ds(first, count)
        weight = head_ref[:, lanes]
        half = jnp.dot(block_ref[...], weight, preferred_element_type=f32)
        t = jnp.tanh(half)
        slope = (1.0 + t) * (1.0 + (half - half * t))
        grad_head = (slope * pooled[:, lanes]).astype(bf16)
        total[...] += contract(grad_head, weight, 1, 1)

    block_copy.wait()
    head_copy.wait()
    chunks(head_ref.shape[1], HEAD_CHUNK, 10, head)
    grad_block = total[...]
    grad_ref[...] = grad_block.astype(bf16)
    gated_copy.wait()
    project_copy.wait()
    project_grad = jnp.dot(grad_block.T.astype(bf16), gated_ref[...], preferred_element_type=f32)
    project_grad_ref[...] = project_grad
    gate_grad_ref[...] = jnp.sum(
        project_ref[...].astype(f32) * project_grad, axis=0, keepdims=True
    )


def backward_kernel(
    place_ref, gate_grad_ref, squeeze_ref, reduce_ref, excite_ref, cells_in, cells_t_in,
    expand_in, depth_ref, half_in, grad_in, project_in, project_grad_in,
    keep_ref, send_ref,
    out_ref,
    cells_ref, cells_t_ref, expand_ref, half_ref, grad_ref, project_ref, gate_row, pool_row,
    expanded, slope, grad_depth, grad_expand, sems,
):
    channels = grad_in.shape[1]
    peers, share, hidden = keep_ref.shape
    half_rows = peers * share
    depth_base = channels
    excite_base = channels + depth_ref.shape[0]
    project_base = half_rows
    reduce_base = half_rows + channels
    arriving = started(
        (cells_in, cells_ref, sems.at[0]),
        (expand_in, expand_ref, sems.at[1]),
        (grad_in, grad_ref, sems.at[2]),
        (project_in, project_ref, sems.at[3]),
        (half_in, half_ref, sems.at[4]),
        (cells_t_in, cells_t_ref, sems.at[5]),
        (project_grad_in, out_ref.at[project_base:reduce_base, :], sems.at[6]),
    )
    cells = half_ref.shape[0]
    columns = cells // 8
    reduced_rows = reduce_ref.shape[0]
    extent, margin = 5, 2
    cell_total = 4 * cells
    excite_end = excite_base + reduced_rows
    reduce_end = reduce_base + reduced_rows

    squeeze = squeeze_ref[...] / cell_total
    reduced_in, reduced, gate = gate_of(squeeze, reduce_ref[...], excite_ref[...])
    grad_excite = (1.0 - gate) * gate_grad_ref[...]
    sigma = jax.nn.sigmoid(reduced_in)
    grad_reduced = jnp.sum(excite_ref[...] * grad_excite, axis=1, keepdims=True) * (
        sigma * (1.0 + reduced_in * (1.0 - sigma))
    )
    back_pool = jnp.sum(reduce_ref[...] * grad_reduced, axis=0, keepdims=True)
    gate_row[...] = 0.25 * gate
    pool_row[...] = back_pool * (0.25 / cell_total)
    once = jnp.where(place_ref[0] == 0, 1.0, 0.0)
    out_ref[excite_base:excite_end, :] = reduced * (grad_excite * once)
    out_ref[reduce_base:reduce_end, :] = grad_reduced * (squeeze * once)
    for first, last in ((excite_end, half_rows), (reduce_end, 2 * half_rows)):
        if first < last:
            out_ref[first:last, :] = jnp.zeros((last - first, out_ref.shape[1]), f32)
    edge = jnp.zeros((margin, 16, BAND), f32)
    expanded[:margin] = edge
    expanded[margin + columns :] = edge
    grad_depth[:margin] = edge[:, :8]
    grad_depth[margin + columns :] = edge[:, :8]

    for copy in arriving[:2]:
        copy.wait()

    @pl.loop(0, out_ref.shape[1] // BAND)
    def each(step):
        backward_band(
            step, arriving[2:], depth_base, excite_base,
            cells_ref, cells_t_ref, expand_ref, depth_ref, half_ref, grad_ref, project_ref,
            out_ref, gate_row, pool_row, expanded, slope, grad_depth, grad_expand,
        )

    core = place_ref[1]
    mine = pl.ds(pl.multiple_of(core * half_rows, half_rows), half_rows)
    theirs = pl.ds(pl.multiple_of((1 - core) * half_rows, half_rows), half_rows)
    keep_ref[...] = out_ref[mine, :][:, :hidden].reshape(keep_ref.shape)
    send_ref[...] = out_ref[theirs, :][:, :hidden].astype(bf16).reshape(send_ref.shape)


def backward_band(
    step, arriving, depth_base, excite_base,
    cells_ref, cells_t_ref, expand_ref, depth_ref, half_ref, grad_ref, project_ref,
    out_ref, gate_row, pool_row, expanded, slope, grad_depth, grad_expand,
):
    columns = half_ref.shape[0] // 8
    channels = grad_ref.shape[1]
    extent, margin = 5, 2
    start = pl.multiple_of(step * BAND, BAND)
    band = pl.ds(start, BAND)
    gate = gate_row[:, band]
    back_pool = pool_row[:, band]

    @pl.loop(0, columns // WIDE)
    def elements(part):
        rows = pl.ds(pl.multiple_of(part * 16 * WIDE, 16 * WIDE), 16 * WIDE)
        half = jnp.dot(cells_ref[rows, :], expand_ref[:, band], preferred_element_type=f32)
        t = jnp.tanh(half)
        turn = half * t
        expanded[pl.ds(margin + part * WIDE, WIDE)] = (half + turn).reshape(WIDE, 16, BAND)
        value = (1.0 + t) * (1.0 + (half - turn))
        slope[pl.ds(part * WIDE, WIDE)] = value.reshape(WIDE, 16, BAND)

    @pl.when(step == 0)
    def arrive():
        for copy in arriving:
            copy.wait()

    @pl.loop(0, columns // WIDE)
    def gradients(part):
        rows = pl.ds(pl.multiple_of(part * 8 * WIDE, 8 * WIDE), 8 * WIDE)
        grad_gated = jnp.dot(
            grad_ref[rows, :], project_ref[:, band], preferred_element_type=f32
        )
        half = half_ref[rows, band]
        t = jnp.tanh(half)
        value = (grad_gated * gate + back_pool) * ((1.0 + t) * (1.0 + (half - half * t)))
        grad_depth[pl.ds(margin + part * WIDE, WIDE)] = value.reshape(WIDE, 8, BAND)

    place = lax.broadcasted_iota(jnp.int32, (8, LANES), 0)

    @pl.loop(0, BAND // LANES)
    def convolve(tile):
        lanes = pl.ds(pl.multiple_of(tile * LANES, LANES), LANES)
        out_lanes = pl.ds(pl.multiple_of(start + tile * LANES, LANES), LANES)

        def taps(number, sums):
            sums = [list(line) for line in sums]
            base = margin + number * TAPS
            grads = {}
            for k in range(TAPS):
                window = row_window(
                    expanded[base + k, :8, lanes], expanded[base + k, 8:, lanes], extent, place
                )
                for j in range(extent):
                    place_x = k - j
                    if place_x not in grads:
                        grads[place_x] = grad_depth[base + place_x + margin, :, lanes]
                    for i in range(extent):
                        sums[i][j] = sums[i][j] + window[i] * grads[place_x]
            return tuple(tuple(line) for line in sums)

        zero = jnp.zeros((8, LANES), f32)
        sums = lax.fori_loop(0, columns // TAPS, taps, ((zero,) * extent,) * extent)
        for i in range(extent):
            for j in range(extent):
                row = depth_base + i * extent + j
                out_ref[row : row + 1, out_lanes] = 2.0 * jnp.sum(sums[i][j], axis=0, keepdims=True)
        for row in range(depth_base + extent * extent, excite_base):
            out_ref[row : row + 1, out_lanes] = jnp.zeros((1, LANES), f32)

        weight = [
            [depth_ref[i * extent + j : i * extent + j + 1, out_lanes] for j in range(extent)]
            for i in range(extent)
        ]

        @pl.loop(0, columns // STRIP)
        def spread(number):
            x0 = number * STRIP
            grads = [grad_depth[x0 + k, :, lanes] for k in range(extent - 1)]
            for x in range(STRIP):
                grads.append(grad_depth[x0 + x + extent - 1, :, lanes])
                whole, far = None, None
                for i in range(extent):
                    term = grads[x + extent - 1] * weight[i][0]
                    for j in range(1, extent):
                        term = term + grads[x + extent - 1 - j] * weight[i][j]
                    d = i - margin
                    if d != 0:
                        term = pltpu.roll(term, d % 8, 0)
                        inside = place >= d if d > 0 else place < 8 + d
                        leave = jnp.where(inside, 0.0, term)
                        far = leave if far is None else far + leave
                    whole = term if whole is None else whole + term
                near = whole - far
                near = near * slope[x0 + x, :8, lanes]
                far = far * slope[x0 + x, 8:, lanes]
                rows = pl.ds(pl.multiple_of((x0 + x) * 16, 16), 16)
                grad_expand[rows, lanes] = jnp.concatenate([near, far], axis=0).astype(bf16)

    out_ref[:channels, band] = jnp.dot(
        cells_t_ref[...], grad_expand[...], preferred_element_type=f32
    )


def unpack_kernel(
    core_ref, own_ref, other_ref,
    expand_ref, depth_ref, reduce_ref, excite_ref, project_ref,
):
    channels = expand_ref.shape[1]
    extent = depth_ref.shape[0]
    reduced = excite_ref.shape[0]
    excite_base = up_to(extent * extent, 8)

    def arrange(first, second):
        expand_ref[0] = first[:channels, :]
        project_ref[0] = second[:channels, :]
        for i in range(extent):
            for j in range(extent):
                row = channels + i * extent + j
                depth_ref[i, j] = first[row : row + 1, :]
        for r in range(reduced):
            row = channels + excite_base + r
            excite_ref[r] = first[row : row + 1, :]
            row = channels + r
            reduce_ref[r] = second[row : row + 1, :]

    @pl.when(core_ref[0] == 0)
    def even():
        arrange(own_ref, other_ref)

    @pl.when(core_ref[0] != 0)
    def odd():
        arrange(other_ref, own_ref)


def shards(views, w_expand, w_depth, w_reduce, w_excite, w_project, w_head, w_class):
    own = views[0, 0]
    height, columns, channels = own.shape
    hidden = w_expand.shape[2]
    reduced = w_reduce.shape[2]
    extent = w_depth.shape[1]
    width = w_head.shape[2]
    classes = w_class.shape[2]
    cells = height * columns
    space = lax.axis_size("space")
    broad = up_to(hidden, BAND)
    tall = up_to(reduced, 8)

    up = [(i, i + 1) for i in range(space - 1)]
    down = [(i + 1, i) for i in range(space - 1)]
    before = lax.ppermute(own[height - 2 :], "space", up)
    after = lax.ppermute(own[:2], "space", down)

    fill = broad - hidden
    expand_w = jnp.pad(w_expand[0] * bf16(0.5), ((0, 0), (0, fill)))
    depth_w = jnp.pad(
        w_depth[0].reshape(extent * extent, hidden).astype(f32),
        ((0, up_to(extent * extent, 8) - extent * extent), (0, fill)),
    )
    reduce_t = jnp.pad(w_reduce[0].T.astype(f32), ((0, tall - reduced), (0, fill)))
    excite_w = jnp.pad(w_excite[0].astype(f32), ((0, tall - reduced), (0, fill)))
    class_t = w_class[0].T
    project_t = jnp.pad(w_project[0].T, ((0, 0), (0, fill)))

    depth_rows = depth_w.shape[0]
    cell_rows, cells_t, mine, half, squeeze = pl.pallas_call(
        forward_kernel,
        in_specs=[VMEM] * 5,
        out_specs=[ANY] * 4 + [VMEM],
        out_shape=[
            jax.ShapeDtypeStruct((16 * columns, channels), bf16),
            jax.ShapeDtypeStruct((channels, 16 * columns), bf16),
            jax.ShapeDtypeStruct((cells, channels), bf16),
            jax.ShapeDtypeStruct((cells, broad), f32),
            jax.ShapeDtypeStruct((1, broad), f32),
        ],
        scratch_shapes=[
            pltpu.VMEM((16 * columns, channels), bf16),
            pltpu.VMEM((channels, 16 * columns), bf16),
            pltpu.VMEM((cells, channels), bf16),
            pltpu.VMEM((cells, broad), f32),
            pltpu.VMEM((16 * columns, LANES), f32),
            pltpu.VMEM((16 * columns, LANES), f32),
            pltpu.VMEM((columns + 4, 16, broad), f32),
            pltpu.SemaphoreType.DMA((3 + broad // LANES,)),
        ],
        compiler_params=PARAMS,
        name="expand_depthwise",
    )(own, before, after, expand_w, depth_w)
    squeeze = lax.psum(squeeze, "space")

    ranks = 2 * space
    logits, gated, block = pl.pallas_call(
        head_kernel,
        in_specs=[ANY] + [VMEM] * 3 + [ANY] * 4,
        out_specs=[VMEM, ANY, VMEM],
        out_shape=[
            jax.ShapeDtypeStruct((ranks, 1, up_to(classes, LANES)), f32),
            jax.ShapeDtypeStruct((cells, broad), bf16),
            jax.ShapeDtypeStruct((cells, channels), bf16),
        ],
        scratch_shapes=[
            pltpu.VMEM((cells, broad), f32),
            pltpu.VMEM((cells, broad), bf16),
            pltpu.VMEM((channels, broad), bf16),
            pltpu.VMEM((cells, channels), bf16),
            pltpu.VMEM((channels, width), bf16),
            pltpu.VMEM((classes, width), bf16),
            pltpu.VMEM((1, broad), f32),
            pltpu.VMEM((8, width), f32),
            pltpu.SemaphoreType.DMA((5,)),
            pltpu.SemaphoreType.DMA((cells // 80,)),
        ],
        compiler_params=PARAMS,
        name="project_head",
    )(half, squeeze, reduce_t, excite_w, project_t, mine, w_head[0], class_t)
    logits = lax.all_to_all(logits, ("space", "pipe"), 0, 0, tiled=True)

    def index(name):
        return lax.axis_index(name).astype(jnp.int32).reshape(1)

    grad_block, project_grad, gate_grad = pl.pallas_call(
        head_grad_kernel,
        in_specs=[SMEM, VMEM] + [ANY] * 5,
        out_specs=[VMEM] * 3,
        out_shape=[
            jax.ShapeDtypeStruct((cells, channels), bf16),
            jax.ShapeDtypeStruct((channels, broad), f32),
            jax.ShapeDtypeStruct((1, broad), f32),
        ],
        scratch_shapes=[
            pltpu.VMEM((cells, channels), bf16),
            pltpu.VMEM((cells, broad), bf16),
            pltpu.VMEM((channels, broad), bf16),
            pltpu.VMEM((channels, width), bf16),
            pltpu.VMEM((classes, width), bf16),
            pltpu.VMEM((1, width), f32),
            pltpu.VMEM((cells, channels), f32),
            pltpu.SemaphoreType.DMA((5,)),
        ],
        compiler_params=PARAMS,
        name="head_grad",
    )(index("pipe"), logits, block, gated, project_t, w_head[0], class_t)
    gate_grad = lax.psum(gate_grad, "space")

    peers = lax.axis_size("x") * lax.axis_size("y")
    share = up_to(-(-(channels + depth_rows + tall) // peers), 16)
    half_rows = peers * share
    keep, send = pl.pallas_call(
        backward_kernel,
        in_specs=[SMEM] + [VMEM] * 4 + [ANY] * 3 + [VMEM] + [ANY] * 4,
        out_specs=[VMEM, VMEM],
        out_shape=[
            jax.ShapeDtypeStruct((peers, share, hidden), f32),
            jax.ShapeDtypeStruct((peers, share, hidden), bf16),
        ],
        scratch_shapes=[
            pltpu.VMEM((2 * half_rows, broad), f32),
            pltpu.VMEM((16 * columns, channels), bf16),
            pltpu.VMEM((channels, 16 * columns), bf16),
            pltpu.VMEM((channels, broad), bf16),
            pltpu.VMEM((cells, broad), f32),
            pltpu.VMEM((cells, channels), bf16),
            pltpu.VMEM((channels, broad), bf16),
            pltpu.VMEM((1, broad), f32),
            pltpu.VMEM((1, broad), f32),
            pltpu.VMEM((columns + 4, 16, BAND), f32),
            pltpu.VMEM((columns, 16, BAND), f32),
            pltpu.VMEM((columns + 4, 8, BAND), f32),
            pltpu.VMEM((16 * columns, BAND), bf16),
            pltpu.SemaphoreType.DMA((7,)),
        ],
        compiler_params=PARAMS,
        name="depthwise_grad",
    )(
        jnp.concatenate([index("space"), index("core")]), gate_grad, squeeze, reduce_t, excite_w, cell_rows, cells_t,
        expand_w, depth_w, half, grad_block, project_t, project_grad,
    )

    swap = [(0, 1), (1, 0)]
    both = (keep + lax.ppermute(send, "core", swap).astype(f32)).astype(bf16)
    pieces = lax.all_to_all(both, ("x", "y"), 0, 0, tiled=True)
    piece = jnp.sum(pieces.astype(f32), axis=0)
    for step in (1, 3):
        piece = piece + lax.ppermute(piece, "space", [(i, i ^ step) for i in range(space)])
    copies = jnp.broadcast_to(piece[None], pieces.shape)
    gathered = lax.all_to_all(copies, ("x", "y"), 0, 0, tiled=True)
    remote = lax.ppermute(gathered, "core", swap)
    g_expand, g_depth, g_reduce, g_excite, g_project = pl.pallas_call(
        unpack_kernel,
        in_specs=[SMEM, VMEM, VMEM],
        out_specs=[VMEM] * 5,
        out_shape=[
            jax.ShapeDtypeStruct((1, channels, hidden), f32),
            jax.ShapeDtypeStruct((extent, extent, 1, hidden), f32),
            jax.ShapeDtypeStruct((reduced, 1, hidden), f32),
            jax.ShapeDtypeStruct((reduced, 1, hidden), f32),
            jax.ShapeDtypeStruct((1, channels, hidden), f32),
        ],
        compiler_params=pltpu.CompilerParams(vmem_limit_bytes=24 * 1024 * 1024),
        name="unpack",
    )(index("core"), gathered.reshape(half_rows, hidden), remote.reshape(half_rows, hidden))
    return (
        g_expand,
        g_depth.transpose(2, 0, 1, 3),
        g_reduce.transpose(1, 2, 0),
        g_excite.transpose(1, 0, 2),
        g_project.transpose(0, 2, 1),
    )


def solution(mesh):
    pipe, replica, space = (mesh.shape[name] for name in ("pipe", "replica", "space"))
    side = 1
    while 2 * side * side < replica:
        side *= 2
    fine = Mesh(
        mesh.devices.reshape(pipe, replica // (2 * side), side, 2, space),
        ("pipe", "x", "y", "core", "space"),
    )
    in_specs = (P("pipe", ("x", "y", "core"), "space"),) + (P("pipe"),) * 7
    return jax.shard_map(
        shards, mesh=fine, in_specs=in_specs, out_specs=(P("pipe"),) * 5, check_vma=False
    )
```

```python
import jax
import jax.numpy as jnp
from jax import lax
from jax.experimental import pallas as pl
from jax.experimental.pallas import tpu as pltpu
from jax.sharding import Mesh
from jax.sharding import PartitionSpec as P

loss_scale = 256.0
f32 = jnp.float32
bf16 = jnp.bfloat16
LANES = 128
BAND = 1152
HEAD_CHUNK = 512
STRIP = 100
WIDE = 100
TAPS = 50
VMEM = pl.BlockSpec(memory_space=pltpu.VMEM)
SMEM = pl.BlockSpec(memory_space=pltpu.SMEM)
ANY = pl.BlockSpec(memory_space=pl.ANY)
PARAMS = pltpu.CompilerParams(vmem_limit_bytes=60 * 1024 * 1024)


def up_to(size, multiple):
    return -(-size // multiple) * multiple


def started(*copies):
    made = [pltpu.make_async_copy(*copy) for copy in copies]
    for copy in made:
        copy.start()
    return made


def chunks(width, chunk, unroll, work):
    whole = width // chunk

    @pl.loop(0, whole, unroll=unroll)
    def each(part):
        work(pl.multiple_of(part * chunk, chunk), chunk)

    if width > whole * chunk:
        work(whole * chunk, width - whole * chunk)


def contract(left, right, left_dim, right_dim):
    return lax.dot_general(
        left, right, (((left_dim,), (right_dim,)), ((), ())), preferred_element_type=f32
    )


def row_window(own, rim, extent, place):
    margin = extent // 2
    window = []
    for i in range(extent):
        d = i - margin
        if d == 0:
            window.append(own)
        elif d > 0:
            window.append(pltpu.roll(jnp.where(place < d, rim, own), 8 - d, 0))
        else:
            window.append(pltpu.roll(jnp.where(place >= 8 + d, rim, own), -d, 0))
    return window


def forward_kernel(
    own_ref, before_ref, after_ref, expand_ref, depth_ref,
    cells_out, cells_t_out, mine_out, half_out, squeeze_ref,
    cells_ref, cells_t_ref, mine_ref, half_ref, left, right, expanded, sems,
):
    columns, channels = own_ref.shape[1:]
    extent, margin = 5, 2

    left[...] = jnp.zeros_like(left)
    right[...] = jnp.zeros_like(right)
    rest = channels - LANES
    for ref, base in ((own_ref, 0), (after_ref, 8), (before_ref, 14)):
        for y in range(ref.shape[0]):
            row = ref[y].astype(f32)
            left[pl.ds(base + y, columns, stride=16), :] = row[:, :LANES]
            right[pl.ds(base + y, columns, stride=16), :] = jnp.concatenate(
                [row[:, LANES:], jnp.zeros((columns, LANES - rest), f32)], axis=1
            )
    low, high = left[...], right[...]
    cells_ref[:, :LANES] = low.astype(bf16)
    cells_ref[:, LANES:] = high[:, :rest].astype(bf16)
    for start in range(0, 16 * columns, 320):
        cells_t_ref[:LANES, start : start + 320] = left[start : start + 320, :].T.astype(bf16)
        cells_t_ref[LANES:, start : start + 320] = right[start : start + 320, :].T[:rest].astype(
            bf16
        )
    mine_ref[:, :LANES] = (
        low.reshape(columns, 16, LANES)[:, :8].reshape(8 * columns, LANES).astype(bf16)
    )
    mine_ref[:, LANES:] = (
        high.reshape(columns, 16, LANES)[:, :8]
        .reshape(8 * columns, LANES)[:, :rest]
        .astype(bf16)
    )
    sends = started(
        (cells_ref, cells_out, sems.at[0]),
        (cells_t_ref, cells_t_out, sems.at[1]),
        (mine_ref, mine_out, sems.at[2]),
    )
    edge = jnp.zeros((margin, 16, expanded.shape[2]), f32)
    expanded[:margin] = edge
    expanded[margin + columns :] = edge

    @pl.loop(0, columns // WIDE)
    def expand(part):
        rows = pl.ds(pl.multiple_of(part * 16 * WIDE, 16 * WIDE), 16 * WIDE)
        half = jnp.dot(cells_ref[rows, :], expand_ref[...], preferred_element_type=f32)
        value = half + half * jnp.tanh(half)
        expanded[pl.ds(margin + part * WIDE, WIDE)] = value.reshape(WIDE, 16, half.shape[1])

    place = lax.broadcasted_iota(jnp.int32, (8, LANES), 0)

    @pl.loop(0, expanded.shape[2] // LANES)
    def convolve(tile):
        lanes = pl.ds(pl.multiple_of(tile * LANES, LANES), LANES)
        weight = [
            [depth_ref[i * extent + j : i * extent + j + 1, lanes] for j in range(extent)]
            for i in range(extent)
        ]

        def strip(number, total):
            x0 = number * STRIP
            sums = {}
            for k in range(STRIP + extent - 1):
                window = row_window(
                    expanded[x0 + k, :8, lanes], expanded[x0 + k, 8:, lanes], extent, place
                )
                for j in range(extent):
                    x = k - j
                    if 0 <= x < STRIP:
                        term = window[0] * weight[0][j]
                        for i in range(1, extent):
                            term = term + window[i] * weight[i][j]
                        sums[x] = term if x not in sums else sums[x] + term
                x = k - extent + 1
                if x >= 0:
                    half = 0.5 * sums.pop(x)
                    half_ref[pl.ds(pl.multiple_of((x0 + x) * 8, 8), 8), lanes] = half
                    total = total + (half + half * jnp.tanh(half))
            return total

        total = lax.fori_loop(0, columns // STRIP, strip, jnp.zeros((8, LANES), f32))
        squeeze_ref[:, lanes] = jnp.sum(total, axis=0, keepdims=True)
        pltpu.make_async_copy(
            half_ref.at[:, lanes], half_out.at[:, lanes], sems.at[3 + tile]
        ).start()

    for tile in range(half_ref.shape[1] // LANES):
        lanes = slice(tile * LANES, (tile + 1) * LANES)
        pltpu.make_async_copy(
            half_ref.at[:, lanes], half_out.at[:, lanes], sems.at[3 + tile]
        ).wait()
    for send in sends:
        send.wait()


def gate_of(squeeze, reduce_t, excite):
    reduced_in = jnp.sum(reduce_t * squeeze, axis=1, keepdims=True)
    reduced = reduced_in * jax.nn.sigmoid(reduced_in)
    gate = jax.nn.sigmoid(jnp.sum(excite * reduced, axis=0, keepdims=True))
    return reduced_in, reduced, gate


def head_kernel(
    half_in, squeeze_ref, reduce_ref, excite_ref, project_in, mine_in, head_in, class_in,
    logits_ref, gated_out, block_ref,
    half_ref, gated_ref, project_ref, mine_ref, head_ref, class_ref, gate_row, sums,
    sems, part_sems,
):
    cells = half_ref.shape[0]
    classes = class_ref.shape[0]

    def piece(part):
        rows = pl.ds(pl.multiple_of(part * 80, 80), 80)
        return half_in.at[rows, :], half_ref.at[rows, :], part_sems.at[part]

    for part in range(cells // 80):
        started(piece(part))
    project_copy, mine_copy, head_copy, class_copy = started(
        (project_in, project_ref, sems.at[3]),
        (mine_in, mine_ref, sems.at[4]),
        (head_in, head_ref, sems.at[0]),
        (class_in, class_ref, sems.at[1]),
    )
    cell_total = 4 * cells
    gate_row[...] = gate_of(squeeze_ref[...] / cell_total, reduce_ref[...], excite_ref[...])[2]

    @pl.loop(0, cells // 80)
    def gating(part):
        pltpu.make_async_copy(*piece(part)).wait()
        rows = pl.ds(pl.multiple_of(part * 80, 80), 80)
        half = half_ref[rows, :]
        gated_ref[rows, :] = ((half + half * jnp.tanh(half)) * gate_row[...]).astype(bf16)

    (send,) = started((gated_ref, gated_out, sems.at[2]))
    project_copy.wait()
    mine_copy.wait()
    residual = contract(gated_ref[...], project_ref[...], 1, 1)
    block = (mine_ref[...].astype(f32) + residual).astype(bf16)
    block_ref[...] = (0.5 * block.astype(f32)).astype(bf16)

    def head(first, count):
        lanes = pl.ds(first, count)
        half = jnp.dot(block_ref[...], head_ref[:, lanes], preferred_element_type=f32)
        act = half + half * jnp.tanh(half)
        sums[:, lanes] = jnp.sum(act.reshape(cells // 8, 8, count), axis=0)

    head_copy.wait()
    chunks(head_ref.shape[1], HEAD_CHUNK, 5, head)
    class_copy.wait()
    pooled = sums[...]
    high = pooled.astype(bf16).astype(f32)
    both = jnp.concatenate([high, pooled - high], axis=0).astype(bf16)
    partial = jnp.sum(contract(both, class_ref[...], 1, 1), axis=0, keepdims=True)
    logits_ref[...] = jnp.zeros_like(logits_ref)
    for rank in range(logits_ref.shape[0]):
        logits_ref[rank, :, :classes] = partial / cell_total
    send.wait()


def head_grad_kernel(
    which_ref, logits_ref, block_in, gated_in, project_in, head_in, class_in,
    grad_ref, project_grad_ref, gate_grad_ref,
    block_ref, gated_ref, project_ref, head_ref, class_ref, pooled, total, sems,
):
    class_copy, block_copy, head_copy, gated_copy, project_copy = started(
        (class_in, class_ref, sems.at[0]),
        (block_in, block_ref, sems.at[1]),
        (head_in, head_ref, sems.at[2]),
        (gated_in, gated_ref, sems.at[3]),
        (project_in, project_ref, sems.at[4]),
    )
    cells = block_ref.shape[0]
    classes = class_ref.shape[0]
    total[...] = jnp.zeros_like(total)

    ranks, wide = logits_ref.shape[0], logits_ref.shape[2]
    valid = lax.broadcasted_iota(jnp.int32, (1, wide), 1) < classes
    teacher, student = logits_ref[0], logits_ref[1]
    for rank in range(2, ranks, 2):
        teacher = teacher + logits_ref[rank]
        student = student + logits_ref[rank + 1]
    exp_teacher = jnp.where(valid, jnp.exp(teacher), 0.0)
    prob = exp_teacher / jnp.sum(exp_teacher, axis=1, keepdims=True)
    log_sum = jnp.log(
        jnp.sum(jnp.where(valid, jnp.exp(student), 0.0), axis=1, keepdims=True)
    )
    logprob = student - log_sum
    cross = jnp.sum(prob * logprob, axis=1, keepdims=True)
    teacher_grad = loss_scale * prob * (cross - logprob)
    student_grad = loss_scale * (jnp.exp(logprob) - prob)
    grad = jnp.where(which_ref[0] == 0, teacher_grad, student_grad)
    grad = jnp.where(valid, grad, 0.0)
    grad = jnp.broadcast_to(grad, (16, wide)).astype(bf16)[:, :classes]
    class_copy.wait()
    pooled[...] = contract(grad, class_ref[...], 1, 0)[:1] * (0.5 / (4 * cells))

    def head(first, count):
        lanes = pl.ds(first, count)
        weight = head_ref[:, lanes]
        half = jnp.dot(block_ref[...], weight, preferred_element_type=f32)
        t = jnp.tanh(half)
        slope = (1.0 + t) * (1.0 + (half - half * t))
        grad_head = (slope * pooled[:, lanes]).astype(bf16)
        total[...] += contract(grad_head, weight, 1, 1)

    block_copy.wait()
    head_copy.wait()
    chunks(head_ref.shape[1], HEAD_CHUNK, 10, head)
    grad_block = total[...]
    grad_ref[...] = grad_block.astype(bf16)
    gated_copy.wait()
    project_copy.wait()
    project_grad = jnp.dot(grad_block.T.astype(bf16), gated_ref[...], preferred_element_type=f32)
    project_grad_ref[...] = project_grad
    gate_grad_ref[...] = jnp.sum(
        project_ref[...].astype(f32) * project_grad, axis=0, keepdims=True
    )


def backward_kernel(
    place_ref, gate_grad_ref, squeeze_ref, reduce_ref, excite_ref, cells_in, cells_t_in,
    expand_in, depth_ref, half_in, grad_in, project_in, project_grad_in,
    keep_ref, send_ref,
    out_ref,
    cells_ref, cells_t_ref, expand_ref, half_ref, grad_ref, project_ref, gate_row, pool_row,
    expanded, slope, grad_depth, grad_expand, sems,
):
    channels = grad_in.shape[1]
    peers, share, hidden = keep_ref.shape
    half_rows = peers * share
    depth_base = channels
    excite_base = channels + depth_ref.shape[0]
    project_base = half_rows
    reduce_base = half_rows + channels
    arriving = started(
        (cells_in, cells_ref, sems.at[0]),
        (expand_in, expand_ref, sems.at[1]),
        (grad_in, grad_ref, sems.at[2]),
        (project_in, project_ref, sems.at[3]),
        (half_in, half_ref, sems.at[4]),
        (cells_t_in, cells_t_ref, sems.at[5]),
        (project_grad_in, out_ref.at[project_base:reduce_base, :], sems.at[6]),
    )
    cells = half_ref.shape[0]
    columns = cells // 8
    reduced_rows = reduce_ref.shape[0]
    extent, margin = 5, 2
    cell_total = 4 * cells
    excite_end = excite_base + reduced_rows
    reduce_end = reduce_base + reduced_rows

    squeeze = squeeze_ref[...] / cell_total
    reduced_in, reduced, gate = gate_of(squeeze, reduce_ref[...], excite_ref[...])
    grad_excite = (1.0 - gate) * gate_grad_ref[...]
    sigma = jax.nn.sigmoid(reduced_in)
    grad_reduced = jnp.sum(excite_ref[...] * grad_excite, axis=1, keepdims=True) * (
        sigma * (1.0 + reduced_in * (1.0 - sigma))
    )
    back_pool = jnp.sum(reduce_ref[...] * grad_reduced, axis=0, keepdims=True)
    gate_row[...] = 0.25 * gate
    pool_row[...] = back_pool * (0.25 / cell_total)
    once = jnp.where(place_ref[0] == 0, 1.0, 0.0)
    out_ref[excite_base:excite_end, :] = reduced * (grad_excite * once)
    out_ref[reduce_base:reduce_end, :] = grad_reduced * (squeeze * once)
    for first, last in ((excite_end, half_rows), (reduce_end, 2 * half_rows)):
        if first < last:
            out_ref[first:last, :] = jnp.zeros((last - first, out_ref.shape[1]), f32)
    edge = jnp.zeros((margin, 16, BAND), f32)
    expanded[:margin] = edge
    expanded[margin + columns :] = edge
    grad_depth[:margin] = edge[:, :8]
    grad_depth[margin + columns :] = edge[:, :8]

    for copy in arriving[:2]:
        copy.wait()

    @pl.loop(0, out_ref.shape[1] // BAND)
    def each(step):
        backward_band(
            step, arriving[2:], depth_base, excite_base,
            cells_ref, cells_t_ref, expand_ref, depth_ref, half_ref, grad_ref, project_ref,
            out_ref, gate_row, pool_row, expanded, slope, grad_depth, grad_expand,
        )

    core = place_ref[1]
    mine = pl.ds(pl.multiple_of(core * half_rows, half_rows), half_rows)
    theirs = pl.ds(pl.multiple_of((1 - core) * half_rows, half_rows), half_rows)
    keep_ref[...] = out_ref[mine, :][:, :hidden].astype(bf16).reshape(keep_ref.shape)
    send_ref[...] = out_ref[theirs, :][:, :hidden].astype(bf16).reshape(send_ref.shape)


def backward_band(
    step, arriving, depth_base, excite_base,
    cells_ref, cells_t_ref, expand_ref, depth_ref, half_ref, grad_ref, project_ref,
    out_ref, gate_row, pool_row, expanded, slope, grad_depth, grad_expand,
):
    columns = half_ref.shape[0] // 8
    channels = grad_ref.shape[1]
    extent, margin = 5, 2
    start = pl.multiple_of(step * BAND, BAND)
    band = pl.ds(start, BAND)
    gate = gate_row[:, band]
    back_pool = pool_row[:, band]

    @pl.loop(0, columns // WIDE)
    def elements(part):
        rows = pl.ds(pl.multiple_of(part * 16 * WIDE, 16 * WIDE), 16 * WIDE)
        half = jnp.dot(cells_ref[rows, :], expand_ref[:, band], preferred_element_type=f32)
        t = jnp.tanh(half)
        turn = half * t
        expanded[pl.ds(margin + part * WIDE, WIDE)] = (half + turn).reshape(WIDE, 16, BAND)
        value = (1.0 + t) * (1.0 + (half - turn))
        slope[pl.ds(part * WIDE, WIDE)] = value.reshape(WIDE, 16, BAND)

    @pl.when(step == 0)
    def arrive():
        for copy in arriving:
            copy.wait()

    @pl.loop(0, columns // WIDE)
    def gradients(part):
        rows = pl.ds(pl.multiple_of(part * 8 * WIDE, 8 * WIDE), 8 * WIDE)
        grad_gated = jnp.dot(
            grad_ref[rows, :], project_ref[:, band], preferred_element_type=f32
        )
        half = half_ref[rows, band]
        t = jnp.tanh(half)
        value = (grad_gated * gate + back_pool) * ((1.0 + t) * (1.0 + (half - half * t)))
        grad_depth[pl.ds(margin + part * WIDE, WIDE)] = value.reshape(WIDE, 8, BAND)

    place = lax.broadcasted_iota(jnp.int32, (8, LANES), 0)

    @pl.loop(0, BAND // LANES)
    def convolve(tile):
        lanes = pl.ds(pl.multiple_of(tile * LANES, LANES), LANES)
        out_lanes = pl.ds(pl.multiple_of(start + tile * LANES, LANES), LANES)

        def taps(number, sums):
            sums = [list(line) for line in sums]
            base = margin + number * TAPS
            grads = {}
            for k in range(TAPS):
                window = row_window(
                    expanded[base + k, :8, lanes], expanded[base + k, 8:, lanes], extent, place
                )
                for j in range(extent):
                    place_x = k - j
                    if place_x not in grads:
                        grads[place_x] = grad_depth[base + place_x + margin, :, lanes]
                    for i in range(extent):
                        sums[i][j] = sums[i][j] + window[i] * grads[place_x]
            return tuple(tuple(line) for line in sums)

        zero = jnp.zeros((8, LANES), f32)
        sums = lax.fori_loop(0, columns // TAPS, taps, ((zero,) * extent,) * extent)
        for i in range(extent):
            for j in range(extent):
                row = depth_base + i * extent + j
                out_ref[row : row + 1, out_lanes] = 2.0 * jnp.sum(sums[i][j], axis=0, keepdims=True)
        for row in range(depth_base + extent * extent, excite_base):
            out_ref[row : row + 1, out_lanes] = jnp.zeros((1, LANES), f32)

        weight = [
            [depth_ref[i * extent + j : i * extent + j + 1, out_lanes] for j in range(extent)]
            for i in range(extent)
        ]

        @pl.loop(0, columns // STRIP)
        def spread(number):
            x0 = number * STRIP
            grads = [grad_depth[x0 + k, :, lanes] for k in range(extent - 1)]
            for x in range(STRIP):
                grads.append(grad_depth[x0 + x + extent - 1, :, lanes])
                whole, far = None, None
                for i in range(extent):
                    term = grads[x + extent - 1] * weight[i][0]
                    for j in range(1, extent):
                        term = term + grads[x + extent - 1 - j] * weight[i][j]
                    d = i - margin
                    if d != 0:
                        term = pltpu.roll(term, d % 8, 0)
                        inside = place >= d if d > 0 else place < 8 + d
                        leave = jnp.where(inside, 0.0, term)
                        far = leave if far is None else far + leave
                    whole = term if whole is None else whole + term
                near = whole - far
                near = near * slope[x0 + x, :8, lanes]
                far = far * slope[x0 + x, 8:, lanes]
                rows = pl.ds(pl.multiple_of((x0 + x) * 16, 16), 16)
                grad_expand[rows, lanes] = jnp.concatenate([near, far], axis=0).astype(bf16)

    out_ref[:channels, band] = jnp.dot(
        cells_t_ref[...], grad_expand[...], preferred_element_type=f32
    )


def unpack_kernel(
    core_ref, own_ref, other_ref,
    expand_ref, depth_ref, reduce_ref, excite_ref, project_ref,
):
    channels = expand_ref.shape[1]
    extent = depth_ref.shape[0]
    reduced = excite_ref.shape[0]
    excite_base = up_to(extent * extent, 8)

    def arrange(first, second):
        expand_ref[0] = first[:channels, :]
        project_ref[0] = second[:channels, :]
        for i in range(extent):
            for j in range(extent):
                row = channels + i * extent + j
                depth_ref[i, j] = first[row : row + 1, :]
        for r in range(reduced):
            row = channels + excite_base + r
            excite_ref[r] = first[row : row + 1, :]
            row = channels + r
            reduce_ref[r] = second[row : row + 1, :]

    @pl.when(core_ref[0] == 0)
    def even():
        arrange(own_ref, other_ref)

    @pl.when(core_ref[0] != 0)
    def odd():
        arrange(other_ref, own_ref)


def shards(views, w_expand, w_depth, w_reduce, w_excite, w_project, w_head, w_class):
    own = views[0, 0]
    height, columns, channels = own.shape
    hidden = w_expand.shape[2]
    reduced = w_reduce.shape[2]
    extent = w_depth.shape[1]
    width = w_head.shape[2]
    classes = w_class.shape[2]
    cells = height * columns
    space = lax.axis_size("space")
    broad = up_to(hidden, BAND)
    tall = up_to(reduced, 8)

    up = [(i, i + 1) for i in range(space - 1)]
    down = [(i + 1, i) for i in range(space - 1)]
    before = lax.ppermute(own[height - 2 :], "space", up)
    after = lax.ppermute(own[:2], "space", down)

    fill = broad - hidden
    expand_w = jnp.pad(w_expand[0] * bf16(0.5), ((0, 0), (0, fill)))
    depth_w = jnp.pad(
        w_depth[0].reshape(extent * extent, hidden).astype(f32),
        ((0, up_to(extent * extent, 8) - extent * extent), (0, fill)),
    )
    reduce_t = jnp.pad(w_reduce[0].T.astype(f32), ((0, tall - reduced), (0, fill)))
    excite_w = jnp.pad(w_excite[0].astype(f32), ((0, tall - reduced), (0, fill)))
    class_t = w_class[0].T
    project_t = jnp.pad(w_project[0].T, ((0, 0), (0, fill)))

    depth_rows = depth_w.shape[0]
    cell_rows, cells_t, mine, half, squeeze = pl.pallas_call(
        forward_kernel,
        in_specs=[VMEM] * 5,
        out_specs=[ANY] * 4 + [VMEM],
        out_shape=[
            jax.ShapeDtypeStruct((16 * columns, channels), bf16),
            jax.ShapeDtypeStruct((channels, 16 * columns), bf16),
            jax.ShapeDtypeStruct((cells, channels), bf16),
            jax.ShapeDtypeStruct((cells, broad), f32),
            jax.ShapeDtypeStruct((1, broad), f32),
        ],
        scratch_shapes=[
            pltpu.VMEM((16 * columns, channels), bf16),
            pltpu.VMEM((channels, 16 * columns), bf16),
            pltpu.VMEM((cells, channels), bf16),
            pltpu.VMEM((cells, broad), f32),
            pltpu.VMEM((16 * columns, LANES), f32),
            pltpu.VMEM((16 * columns, LANES), f32),
            pltpu.VMEM((columns + 4, 16, broad), f32),
            pltpu.SemaphoreType.DMA((3 + broad // LANES,)),
        ],
        compiler_params=PARAMS,
        name="expand_depthwise",
    )(own, before, after, expand_w, depth_w)
    squeeze = lax.psum(squeeze, "space")

    ranks = 2 * space
    logits, gated, block = pl.pallas_call(
        head_kernel,
        in_specs=[ANY] + [VMEM] * 3 + [ANY] * 4,
        out_specs=[VMEM, ANY, VMEM],
        out_shape=[
            jax.ShapeDtypeStruct((ranks, 1, up_to(classes, LANES)), f32),
            jax.ShapeDtypeStruct((cells, broad), bf16),
            jax.ShapeDtypeStruct((cells, channels), bf16),
        ],
        scratch_shapes=[
            pltpu.VMEM((cells, broad), f32),
            pltpu.VMEM((cells, broad), bf16),
            pltpu.VMEM((channels, broad), bf16),
            pltpu.VMEM((cells, channels), bf16),
            pltpu.VMEM((channels, width), bf16),
            pltpu.VMEM((classes, width), bf16),
            pltpu.VMEM((1, broad), f32),
            pltpu.VMEM((8, width), f32),
            pltpu.SemaphoreType.DMA((5,)),
            pltpu.SemaphoreType.DMA((cells // 80,)),
        ],
        compiler_params=PARAMS,
        name="project_head",
    )(half, squeeze, reduce_t, excite_w, project_t, mine, w_head[0], class_t)
    logits = lax.all_to_all(logits, ("space", "pipe"), 0, 0, tiled=True)

    def index(name):
        return lax.axis_index(name).astype(jnp.int32).reshape(1)

    grad_block, project_grad, gate_grad = pl.pallas_call(
        head_grad_kernel,
        in_specs=[SMEM, VMEM] + [ANY] * 5,
        out_specs=[VMEM] * 3,
        out_shape=[
            jax.ShapeDtypeStruct((cells, channels), bf16),
            jax.ShapeDtypeStruct((channels, broad), f32),
            jax.ShapeDtypeStruct((1, broad), f32),
        ],
        scratch_shapes=[
            pltpu.VMEM((cells, channels), bf16),
            pltpu.VMEM((cells, broad), bf16),
            pltpu.VMEM((channels, broad), bf16),
            pltpu.VMEM((channels, width), bf16),
            pltpu.VMEM((classes, width), bf16),
            pltpu.VMEM((1, width), f32),
            pltpu.VMEM((cells, channels), f32),
            pltpu.SemaphoreType.DMA((5,)),
        ],
        compiler_params=PARAMS,
        name="head_grad",
    )(index("pipe"), logits, block, gated, project_t, w_head[0], class_t)
    gate_grad = lax.psum(gate_grad, "space")

    peers = lax.axis_size("x") * lax.axis_size("y")
    share = up_to(-(-(channels + depth_rows + tall) // peers), 16)
    half_rows = peers * share
    keep, send = pl.pallas_call(
        backward_kernel,
        in_specs=[SMEM] + [VMEM] * 4 + [ANY] * 3 + [VMEM] + [ANY] * 4,
        out_specs=[VMEM, VMEM],
        out_shape=[
            jax.ShapeDtypeStruct((peers, share, hidden), bf16),
            jax.ShapeDtypeStruct((peers, share, hidden), bf16),
        ],
        scratch_shapes=[
            pltpu.VMEM((2 * half_rows, broad), f32),
            pltpu.VMEM((16 * columns, channels), bf16),
            pltpu.VMEM((channels, 16 * columns), bf16),
            pltpu.VMEM((channels, broad), bf16),
            pltpu.VMEM((cells, broad), f32),
            pltpu.VMEM((cells, channels), bf16),
            pltpu.VMEM((channels, broad), bf16),
            pltpu.VMEM((1, broad), f32),
            pltpu.VMEM((1, broad), f32),
            pltpu.VMEM((columns + 4, 16, BAND), f32),
            pltpu.VMEM((columns, 16, BAND), f32),
            pltpu.VMEM((columns + 4, 8, BAND), f32),
            pltpu.VMEM((16 * columns, BAND), bf16),
            pltpu.SemaphoreType.DMA((7,)),
        ],
        compiler_params=PARAMS,
        name="depthwise_grad",
    )(
        jnp.concatenate([index("space"), index("core")]), gate_grad, squeeze, reduce_t, excite_w, cell_rows, cells_t,
        expand_w, depth_w, half, grad_block, project_t, project_grad,
    )

    swap = [(0, 1), (1, 0)]
    received = lax.ppermute(send, "core", swap)
    both = (keep.astype(f32) + received.astype(f32)).astype(bf16)
    pieces = lax.all_to_all(both, ("x", "y"), 0, 0, tiled=True)
    piece = jnp.sum(pieces.astype(f32), axis=0)
    for step in (1, 3):
        piece = piece + lax.ppermute(piece, "space", [(i, i ^ step) for i in range(space)])
    copies = jnp.broadcast_to(piece[None], pieces.shape)
    gathered = lax.all_to_all(copies, ("x", "y"), 0, 0, tiled=True)
    remote = lax.ppermute(gathered, "core", swap)
    g_expand, g_depth, g_reduce, g_excite, g_project = pl.pallas_call(
        unpack_kernel,
        in_specs=[SMEM, VMEM, VMEM],
        out_specs=[VMEM] * 5,
        out_shape=[
            jax.ShapeDtypeStruct((1, channels, hidden), f32),
            jax.ShapeDtypeStruct((extent, extent, 1, hidden), f32),
            jax.ShapeDtypeStruct((reduced, 1, hidden), f32),
            jax.ShapeDtypeStruct((reduced, 1, hidden), f32),
            jax.ShapeDtypeStruct((1, channels, hidden), f32),
        ],
        compiler_params=pltpu.CompilerParams(vmem_limit_bytes=24 * 1024 * 1024),
        name="unpack",
    )(index("core"), gathered.reshape(half_rows, hidden), remote.reshape(half_rows, hidden))
    return (
        g_expand,
        g_depth.transpose(2, 0, 1, 3),
        g_reduce.transpose(1, 2, 0),
        g_excite.transpose(1, 0, 2),
        g_project.transpose(0, 2, 1),
    )


def solution(mesh):
    pipe, replica, space = (mesh.shape[name] for name in ("pipe", "replica", "space"))
    side = 1
    while 2 * side * side < replica:
        side *= 2
    fine = Mesh(
        mesh.devices.reshape(pipe, replica // (2 * side), side, 2, space),
        ("pipe", "x", "y", "core", "space"),
    )
    in_specs = (P("pipe", ("x", "y", "core"), "space"),) + (P("pipe"),) * 7
    return jax.shard_map(
        shards, mesh=fine, in_specs=in_specs, out_specs=(P("pipe"),) * 5, check_vma=False
    )
```
